32 devices in a mesh: seq: 8 (over y, x, core), head: 4 (over z).
Axes of the slice: x: 2, y: 2, z: 4, core: 2. Of those that a mesh axis runs over, the one named last changes fastest.
Arguments:
- hidden_in: bfloat16 [2048, 2880], P(('seq', 'head')), may hold values from -16 to 16
- qkv_new: bfloat16 [2048, 8, 640], P(('seq', 'head')), may hold values from -250 to 250
- kv_cache: bfloat16 [8, 8192, 8, 128], P('seq', None, 'head'), may hold values from -4 to 4
- cache_len: int32 [8], P('seq'), may hold values from 2048 to 8192, as said below
- o_weight: bfloat16 [4096, 2880], P('head'), may hold values from -1 to 1
- norm_gain: float32 [2880], replicated, may hold values from 0.1 to 1.9
- expert_ids: int32 [2048, 4], P(('seq', 'head')), may hold values from 0 to 7, all different within a row; in each aligned block of 64 rows (0 to 63, 64 to 127, ...) at most 40 rows name the same one
- gate_weights: float32 [2048, 4], P(('seq', 'head')), may hold values from 0.1 to 1
- w_gate_up: bfloat16 [8, 2880, 2, 2880], P('seq', None, None, 'head'), may hold values from -0.109375 to 0.109375
- w_down: bfloat16 [8, 2880, 2880], P('seq', 'head'), may hold values from -0.109375 to 0.109375
Outputs:
- attn_proj: bfloat16 [2048, 2880], P(('seq', 'head'))
- moe_out: bfloat16 [2048, 2880], P(('seq', 'head'))
The draws below stay inside these ranges and needn't reach their ends.
Inputs may be any that keep to these rules, and one draw needn't show every extreme that they name: `cache_len`: some sequence has exactly 8192 live cached positions in every draw. `expert_ids`: each token names 4 different experts. Among the tokens of one device (aligned blocks of 64 tokens) no expert is named more than 40 times, a bound that some block reaches.
All inputs are finite; a program needn't handle non-finite values.
Results may differ from the reference program's by a relative error of at most 0.024.
Values may be sent and summed in bfloat16 or wider, within the bound.
No kernel may reach another device: no remote copies, remote signals or barrier semaphores. Data moves between devices by JAX's collectives and lax.ppermute only.
A program may use at most 256 MiB of HBM per device.

```python
import math
import jax
import jax.numpy as jnp
import numpy as np
from jax import lax

D = 2880
HD = 64
KVH = 8
GQA = 8
FF = 2880
TOP = 4
NEW_TOK = 256
CACHE = 8192
SEQS = 8
TOKENS = 2048
TOK_DEV = 64
EXPERTS = 8
CAP = 40
N_HEAD = 4
DEVICES = 32


def draw_hidden_in(key, part):
    first, second = jax.random.split(key, 2)
    base = jax.random.truncated_normal(first, -4.0, 4.0, (TOKENS, D), jnp.float32)
    scales = jnp.exp(jax.random.uniform(second, (TOKENS, 1), jnp.float32, math.log(0.3), math.log(3.0)))
    return (base * scales).astype(jnp.bfloat16)


def draw_qkv_new(key, part):
    first = jax.random.fold_in(key, 0)
    base = jax.random.truncated_normal(first, -4.0, 4.0, (TOKENS, KVH, (GQA + 2) * HD), jnp.float32)
    query_part = base[:, :, :GQA * HD] * 2.0
    key_part = base[:, :, GQA * HD:(GQA + 1) * HD]
    value_part = base[:, :, (GQA + 1) * HD:]
    return jnp.concatenate([query_part, key_part, value_part], axis=2).astype(jnp.bfloat16)


def draw_cache_len(key, part):
    first, second = jax.random.split(key)
    lengths = jax.random.randint(first, (SEQS,), CACHE // 4, CACHE + 1, jnp.int32)
    chosen = jax.random.randint(second, (), 0, SEQS, jnp.int32)
    return jnp.where(jnp.arange(SEQS, dtype=jnp.int32) == chosen, CACHE, lengths).astype(jnp.int32)


def levels(stream_key, dims, cuts, low, largest):
    level = 1.0
    for axis_at, parts in cuts:
        heights = jax.random.uniform(jax.random.fold_in(jax.random.fold_in(stream_key, 6), axis_at), (parts,), jnp.float32, low / len(cuts), largest / len(cuts))
        level = level * jnp.repeat(jnp.exp(heights), dims[axis_at] // parts).reshape((-1,) + (1,) * (len(dims) - 1 - axis_at))
    return level


def deal_out(own_key, own, number, rows, count, top, most, slope):
    order = jax.random.permutation(own_key, count)
    packed, ordinary = load_shares(count, rows * top, most, slope, True), load_shares(count, rows * top, most, slope, False)
    places = jnp.arange(count)

    def named(sizes, rotation):
        used = int((sizes > 0).sum())
        fixed = max(1, used // 4)
        shifted = fixed + (places - fixed + rotation * (used - fixed)) % max(1, count - fixed)
        return jnp.zeros((count,), jnp.int32).at[order[jnp.where(places < fixed, places, shifted)]].set(jnp.asarray(sizes, jnp.int32))

    sizes = jnp.where(number % 4 == 0, named(packed, number // 4), named(ordinary, number - number // 4 - 1))
    mixed = jax.random.permutation(jax.random.fold_in(own, 3), count)
    source_of, sink = mixed[0:count // 2 * 2:2], mixed[1:count // 2 * 2:2]
    margin = jnp.minimum(sizes[source_of] - 1, most - sizes[sink]) // 2
    margin = jnp.where((source_of == order[0]) | (sink == order[0]) | (sizes[sink] == 0), 0, jnp.maximum(margin, 0))
    shifted = jax.random.randint(jax.random.fold_in(own, 4), (count // 2,), 0, 1 << 20) % (margin + 1)
    sizes = sizes.at[source_of].add(-shifted).at[sink].add(shifted)
    labels = jnp.searchsorted(jnp.cumsum(sizes), jnp.arange(rows * top), side="right").astype(jnp.int32)
    table = labels.reshape(top, rows).T
    table = table[jax.random.permutation(jax.random.fold_in(own, 1), rows)]
    rotation = jax.random.randint(jax.random.fold_in(own, 2), (rows, 1), 0, top)
    return jnp.take_along_axis(table, (jnp.arange(top)[None, :] + rotation) % top, axis=1)


def load_shares(amount, total, reach, lean, full):
    loads = [(1 << 20) // math.isqrt(rank ** lean) + 1 for rank in range(1, amount + 1)]
    largest = reach if full else min(reach, max(-(-total // amount), total * loads[0] // sum(loads)))
    least = 1 if total - largest >= amount - 1 else 0
    given, spare = [largest] + [least] * (amount - 1), total - largest - least * (amount - 1)
    while spare > 0:
        movable = [i for i in range(1, amount) if given[i] < largest] or [i for i in range(1, amount) if given[i] < reach]
        pool, remaining = sum([loads[i] for i in movable]), spare
        for i in movable:
            addition = min(reach - given[i], max(1, remaining * loads[i] // pool), spare)
            given[i] = given[i] + addition
            spare = spare - addition
    return np.array(given)


def gaussian(own_key, shape, deviation, limit, cuts=(), kind=jnp.bfloat16):
    loudness = levels(own_key, shape, cuts, -0.22, 0.18) if cuts else 1.0
    entries = jax.random.normal(own_key, shape, jnp.float32) * deviation * loudness
    return jnp.minimum(jnp.maximum(entries, -limit), limit).astype(kind)


def setup_inputs(seed: int = 0) -> dict:
    arg_keys = jax.random.split(jax.random.key(seed), 11)
    hidden_in = draw_hidden_in(jax.random.fold_in(arg_keys[10], 71), 0)
    qkv_new = draw_qkv_new(jax.random.fold_in(arg_keys[10], 71), 0)
    kv_cache = gaussian(arg_keys[2], (SEQS, CACHE, KVH, 2 * HD), 1.0, 4.0, ((0, 8), (2, 4)))
    cache_len = draw_cache_len(jax.random.fold_in(arg_keys[10], 71), 0)
    o_weight = gaussian(arg_keys[4], (KVH * GQA * HD, D), 0.2, 1.0, ((0, 4),))
    norm_gain = jnp.clip(1.0 + 0.18 * jax.random.normal(arg_keys[5], (D,), jnp.float32), 0.1, 1.9)
    expert_ids_keys = jax.random.split(jax.random.fold_in(arg_keys[6], 1), TOKENS // TOK_DEV)
    expert_ids_turns = jax.random.permutation(jax.random.fold_in(arg_keys[6], 3), TOKENS // TOK_DEV)
    expert_ids = jax.vmap(lambda own, number: deal_out(jax.random.fold_in(arg_keys[6], 2), own, number, TOK_DEV, EXPERTS, TOP, CAP, 2))(expert_ids_keys, expert_ids_turns).reshape((TOKENS, TOP))
    gate_weights = jnp.clip(0.1 + 0.9 * jax.random.uniform(arg_keys[7], (TOKENS, TOP), jnp.float32) ** levels(arg_keys[7], (TOKENS, TOP), ((0, 32),), -0.2, 0.2), 0.1, 1.0)
    w_gate_up = gaussian(arg_keys[8], (EXPERTS, D, 2, FF), D ** -0.5, 0.109375, ((0, 8), (3, 4)))
    w_down = gaussian(arg_keys[9], (EXPERTS, FF, D), FF ** -0.5, 0.109375, ((0, 8), (1, 4)))
    return dict(hidden_in=hidden_in, qkv_new=qkv_new, kv_cache=kv_cache, cache_len=cache_len, o_weight=o_weight, norm_gain=norm_gain, expert_ids=expert_ids, gate_weights=gate_weights, w_gate_up=w_gate_up, w_down=w_down)


epsilon = 1e-05

def attend(fresh_group, stored, live_len):
    fresh_len = fresh_group.shape[0]
    cached = stored.shape[0]
    head_dim = stored.shape[1] // 2
    group_size = fresh_group.shape[1] // head_dim - 2
    queries = fresh_group[:, :group_size * head_dim].reshape(fresh_len * group_size, head_dim)
    key_rows = jnp.concatenate([stored[:, :head_dim], fresh_group[:, group_size * head_dim:(group_size + 1) * head_dim]], axis=0)
    value_rows = jnp.concatenate([stored[:, head_dim:], fresh_group[:, (group_size + 1) * head_dim:]], axis=0)
    scores = jnp.einsum('qd,kd->qk', queries.astype(jnp.float32), key_rows.astype(jnp.float32)) * head_dim ** (-0.5)
    positions = lax.broadcasted_iota(jnp.int32, scores.shape, 1)
    token_pos = lax.broadcasted_iota(jnp.int32, scores.shape, 0) // group_size
    visible = (positions < live_len) | (positions >= cached) & (positions - cached <= token_pos)
    masked = jnp.where(visible, scores, -jnp.inf)
    row_max = lax.optimization_barrier(jnp.max(masked, axis=1, keepdims=True))
    exponent = jnp.where(visible, jnp.exp(masked - row_max), 0.0)
    weights = (exponent / lax.optimization_barrier(jnp.sum(exponent, axis=1, keepdims=True))).astype(jnp.bfloat16)
    result = jnp.dot(weights, value_rows, preferred_element_type=jnp.float32).astype(jnp.bfloat16)
    return result.reshape(fresh_len, group_size * head_dim)

def slot_numbers(expert_ids):
    flat_ids = expert_ids.reshape(-1, TOK_DEV * TOP)
    onehot = (flat_ids[:, :, None] == jnp.arange(EXPERTS, dtype=jnp.int32)[None, None, :]).astype(jnp.int32)
    before = jnp.cumsum(onehot, axis=1) - onehot
    return lax.optimization_barrier(jnp.sum(before * onehot, axis=2)).reshape(TOKENS, TOP).astype(jnp.int32)

def reference(hidden_in, qkv_new, kv_cache, cache_len, o_weight, norm_gain, expert_ids, gate_weights, w_gate_up, w_down):
    sequences = qkv_new.reshape(SEQS, NEW_TOK, KVH, (GQA + 2) * HD)

    def per_seq(seq_index):
        group_rows = lax.dynamic_index_in_dim(sequences, seq_index, 0, keepdims=False)
        stored_all = lax.dynamic_index_in_dim(kv_cache, seq_index, 0, keepdims=False)
        live_len = lax.dynamic_index_in_dim(cache_len, seq_index, 0, keepdims=False)

        def per_head(head_index):
            fresh_group = lax.dynamic_index_in_dim(group_rows, head_index, 1, keepdims=False)
            stored = lax.dynamic_index_in_dim(stored_all, head_index, 1, keepdims=False)
            return attend(fresh_group, stored, live_len)
        return lax.map(per_head, jnp.arange(KVH, dtype=jnp.int32))
    heads_out = lax.map(per_seq, jnp.arange(SEQS, dtype=jnp.int32))
    attention = jnp.transpose(heads_out, (0, 2, 1, 3)).reshape(TOKENS, KVH * GQA * HD)
    attn_proj = jnp.dot(attention, o_weight, preferred_element_type=jnp.float32).astype(jnp.bfloat16)
    kept_proj = lax.optimization_barrier(attn_proj)
    residual = (hidden_in.astype(jnp.float32) + kept_proj.astype(jnp.float32)).astype(jnp.bfloat16)
    widened = lax.optimization_barrier(residual).astype(jnp.float32)
    normed = (widened * lax.rsqrt(lax.optimization_barrier(jnp.mean(widened * widened, axis=1, keepdims=True)) + epsilon) * norm_gain).astype(jnp.bfloat16)
    slot_ids = slot_numbers(expert_ids)
    blocks = (jnp.arange(TOKENS, dtype=jnp.int32) // TOK_DEV)[:, None]
    dest_rows = (blocks * CAP + slot_ids).astype(jnp.int32)
    buffer = jnp.zeros((EXPERTS, DEVICES * CAP, D), jnp.bfloat16)
    buffer = buffer.at[expert_ids, dest_rows].set(jnp.broadcast_to(normed[:, None, :], (TOKENS, TOP, D)))

    def per_expert(operands):
        slot_rows, pair_weight, down_weight = operands
        gate_up = jnp.dot(slot_rows, pair_weight.reshape(D, 2 * FF), preferred_element_type=jnp.float32)
        hidden = (jax.nn.silu(gate_up[:, :FF]) * gate_up[:, FF:]).astype(jnp.bfloat16)
        pieces = jnp.einsum('rqf,qfd->qrd', hidden.reshape(-1, N_HEAD, FF // N_HEAD).astype(jnp.float32), down_weight.reshape(N_HEAD, FF // N_HEAD, D).astype(jnp.float32))
        rounded = lax.optimization_barrier(pieces.astype(jnp.bfloat16)).astype(jnp.float32)
        return lax.optimization_barrier(jnp.sum(rounded, axis=0)).astype(jnp.bfloat16)
    expert_out = lax.map(per_expert, (buffer, w_gate_up, w_down))
    picked = expert_out[expert_ids, dest_rows].astype(jnp.float32)
    moe_out = lax.optimization_barrier(jnp.sum(picked * gate_weights[:, :, None], axis=1)).astype(jnp.bfloat16)
    return (attn_proj, moe_out)
```

```python
import functools

import jax
import jax.numpy as jnp
from jax import lax
from jax.experimental import pallas as pl
from jax.experimental.pallas import tpu as pltpu
from jax.sharding import PartitionSpec as P

TOP = 4
EPSILON = 1e-05
LOG2E = 1.4426950408889634
FLOOR = -1e30
AXES = ("seq", "head")
MIB = 2**20
VMEM = pltpu.VMEM
SMEM = pltpu.SMEM


def key_block(cached):
    return 2048 if cached % 2048 == 0 else cached


def attend_kernel(
    info, chunk, fresh, cache, o_weight, out, queries, acc, top, o_local, sem, *, tok, hd, gs, bk
):
    heads, cached, _ = cache.shape
    live = info[0]
    mine = info[1]
    asked = info[2]
    o_copy = pltpu.make_async_copy(o_weight, o_local, sem)
    o_copy.start()
    rows = tok * gs
    for h in range(heads):
        for r in range(gs):
            one = chunk[h, :, r * hd : (r + 1) * hd] * jnp.bfloat16(hd**-0.5)
            queries[h, r * tok : (r + 1) * tok, :] = jnp.concatenate(
                [one, jnp.zeros_like(one)], axis=1
            )
    lane = lax.broadcasted_iota(jnp.int32, (1, 2 * hd), 1)
    is_value = (lane >= hd).astype(jnp.float32).astype(jnp.bfloat16)
    is_key = (lane < hd).astype(jnp.float32).astype(jnp.bfloat16)

    def block(h, keys, mask, first):
        scores = lax.dot_general(
            queries[h], keys, (((1,), (1,)), ((), ())), preferred_element_type=jnp.float32
        )
        if mask is not None:
            scores = jnp.where(mask(scores.shape), scores, FLOOR)
        return scores

    def absorb(h, keys, scores, first):
        largest = jnp.max(scores, axis=1, keepdims=True)
        values = keys * is_value + is_key
        if first:
            now = jnp.broadcast_to(largest, top.shape[1:])
        else:
            before = top[h]
            now = jnp.maximum(before, largest)
        weights = jnp.exp2((scores - now[:, :1]) * LOG2E).astype(jnp.bfloat16)
        part = jnp.dot(weights, values, preferred_element_type=jnp.float32)
        if first:
            acc[h] = part
        else:
            acc[h] = acc[h] * jnp.exp2((before - now) * LOG2E) + part
        top[h] = now

    def causal(shape):
        column = lax.broadcasted_iota(jnp.int32, shape, 1)
        row = lax.broadcasted_iota(jnp.int32, shape, 0)
        where = (mine ^ (column // tok)) * tok + column % tok
        return where <= asked * tok + row % tok

    fresh_scores = [block(h, fresh[h], causal, True) for h in range(heads)]
    for h in range(heads):
        absorb(h, fresh[h], fresh_scores[h], True)

    def cached_step(index, masked):
        start = pl.multiple_of(index * bk, bk)
        keys = [cache[h, pl.ds(start, bk), :] for h in range(heads)]

        def alive(shape):
            return lax.broadcasted_iota(jnp.int32, shape, 1) + start < live

        scores = [block(h, keys[h], alive if masked else None, False) for h in range(heads)]
        for h in range(heads):
            absorb(h, keys[h], scores[h], False)

    full = live // bk

    def body(index, carry):
        cached_step(index, False)
        return carry

    lax.fori_loop(0, full, body, 0)

    @pl.when(full * bk < live)
    def _():
        cached_step(full, True)

    parts = []
    for h in range(heads):
        total = acc[h]
        done = (total[:, hd:] / total[:, :hd]).astype(jnp.bfloat16)
        parts += [done[r * tok : (r + 1) * tok] for r in range(gs)]
    attention = jnp.concatenate(parts, axis=1)
    o_copy.wait()
    out[...] = lax.dot_general(
        attention, o_local[...], (((1,), (1,)), ((), ())), preferred_element_type=jnp.float32
    ).astype(out.dtype)


def attend(info, chunk, fresh, cache, o_rows, tok, hd, gs):
    heads, cached, lanes = cache.shape
    width, depth = o_rows.shape
    return pl.pallas_call(
        functools.partial(attend_kernel, tok=tok, hd=hd, gs=gs, bk=key_block(cached)),
        out_shape=jax.ShapeDtypeStruct((tok, width), jnp.bfloat16),
        in_specs=[pl.BlockSpec(memory_space=SMEM)]
        + [pl.BlockSpec(memory_space=VMEM)] * 3
        + [pl.BlockSpec(memory_space=pl.ANY)],
        out_specs=pl.BlockSpec(memory_space=VMEM),
        scratch_shapes=[
            VMEM((heads, tok * gs, lanes), jnp.bfloat16),
            VMEM((heads, tok * gs, lanes), jnp.float32),
            VMEM((heads, tok * gs, 128), jnp.float32),
            VMEM((width, depth), jnp.bfloat16),
            pltpu.SemaphoreType.DMA,
        ],
        compiler_params=pltpu.CompilerParams(vmem_limit_bytes=48 * MIB),
        cost_estimate=pl.CostEstimate(
            flops=16 * heads * tok * gs * cached * hd,
            bytes_accessed=heads * cached * lanes * 2 + width * depth * 2,
            transcendentals=heads * tok * gs * cached,
        ),
        name="attend",
    )(info, chunk, fresh, cache, o_rows)


def norm_kernel(hidden, gain, own, others, proj, normed):
    total = own[...].astype(jnp.float32)
    for k in range(others.shape[0]):
        total = total + others[k].astype(jnp.float32)
    rounded = total.astype(jnp.bfloat16)
    proj[...] = rounded
    residual = (hidden[...].astype(jnp.float32) + rounded.astype(jnp.float32)).astype(jnp.bfloat16)
    wide = residual.astype(jnp.float32)
    mean = jnp.mean(wide * wide, axis=1, keepdims=True)
    normed[...] = (wide * lax.rsqrt(mean + EPSILON) * gain[...]).astype(jnp.bfloat16)


def norm(hidden, gain, own, others):
    shape = jax.ShapeDtypeStruct(hidden.shape, jnp.bfloat16)
    return pl.pallas_call(
        norm_kernel, out_shape=(shape, shape), name="norm",
        compiler_params=pltpu.CompilerParams(vmem_limit_bytes=16 * MIB),
    )(hidden, gain.reshape(1, -1), own, others)


def experts_kernel(
    expert, ids, gates, near, far, w_in, w_down, out_near, out_far, rows, total, chosen, *, steps
):
    step = pl.program_id(0)
    half = near.shape[0]
    count = rows.shape[0]

    @pl.when(step == 0)
    def _():
        picked = jnp.sum((ids[...] == expert[0]).astype(jnp.float32), axis=0, keepdims=True)
        lanes = picked.shape[1]
        earlier = (
            lax.broadcasted_iota(jnp.int32, (lanes, lanes), 0)
            < lax.broadcasted_iota(jnp.int32, (lanes, lanes), 1)
        ).astype(jnp.float32).astype(jnp.bfloat16)
        eight = jnp.broadcast_to(picked, (16, lanes)).astype(jnp.bfloat16)
        slot = jnp.dot(eight, earlier, preferred_element_type=jnp.float32)[:1]
        slot = jnp.where(picked > 0.5, slot, -1.0).astype(jnp.int32)
        places = lax.broadcasted_iota(jnp.int32, (count, lanes), 0) == slot
        chosen[...] = places.astype(jnp.float32).astype(jnp.bfloat16)
        got = jnp.dot(chosen[:, :half], near[...], preferred_element_type=jnp.float32)
        got = got + jnp.dot(chosen[:, half:], far[...], preferred_element_type=jnp.float32)
        rows[...] = got.astype(jnp.bfloat16)

    contract_last = (((1,), (1,)), ((), ()))
    gate = lax.dot_general(rows[...], w_in[0], contract_last, preferred_element_type=jnp.float32)
    up = lax.dot_general(rows[...], w_in[1], contract_last, preferred_element_type=jnp.float32)
    hidden = (gate / (1.0 + jnp.exp(-gate)) * up).astype(jnp.bfloat16)
    part = jnp.dot(hidden, w_down[...], preferred_element_type=jnp.float32)

    @pl.when(step == 0)
    def _():
        total[...] = part

    @pl.when(step > 0)
    def _():
        total[...] += part

    @pl.when(step == steps - 1)
    def _():
        weight = jnp.sum(
            jnp.where(ids[...] == expert[0], gates[...], 0.0), axis=0, keepdims=True
        )
        wide = chosen[...].astype(jnp.float32)
        per_row = jnp.sum(wide * weight, axis=1, keepdims=True)
        scaled = (total[...] * per_row).astype(jnp.bfloat16)
        first = (((0,), (0,)), ((), ()))
        out_near[...] = lax.dot_general(
            chosen[:, :half], scaled, first, preferred_element_type=jnp.float32
        ).astype(jnp.bfloat16)
        out_far[...] = lax.dot_general(
            chosen[:, half:], scaled, first, preferred_element_type=jnp.float32
        ).astype(jnp.bfloat16)


def run_experts(expert, ids, gates, near, far, w_in, w_down, count):
    half, width = near.shape
    units = w_down.shape[0]
    steps = 3 if units % 48 == 0 else 1
    part = units // steps
    whole = lambda shape: pl.BlockSpec(
        shape, lambda i: (0,) * len(shape), pipeline_mode=pl.Buffered(1)
    )
    shape = jax.ShapeDtypeStruct((half, width), jnp.bfloat16)
    return pl.pallas_call(
        functools.partial(experts_kernel, steps=steps),
        out_shape=(shape, shape),
        grid=(steps,),
        in_specs=[
            pl.BlockSpec(memory_space=SMEM),
            whole(ids.shape),
            whole(gates.shape),
            whole(near.shape),
            whole(far.shape),
            pl.BlockSpec((2, part, width), lambda i: (0, i, 0)),
            pl.BlockSpec((part, width), lambda i: (i, 0)),
        ],
        out_specs=(whole(near.shape), whole(far.shape)),
        scratch_shapes=[
            VMEM((count, width), jnp.bfloat16),
            VMEM((count, width), jnp.float32),
            VMEM((count, 2 * half), jnp.bfloat16),
        ],
        compiler_params=pltpu.CompilerParams(vmem_limit_bytes=52 * MIB),
        cost_estimate=pl.CostEstimate(
            flops=2 * count * width * (units * 3 + 4 * half),
            bytes_accessed=units * width * 6 + half * width * 8,
            transcendentals=count * units,
        ),
        name="experts",
    )(expert, ids, gates, near, far, w_in, w_down)


def per_device(
    hidden_in, qkv_new, kv_cache, cache_len, o_weight, norm_gain,
    expert_ids, gate_weights, w_gate_up, w_down,
):
    seqs = lax.axis_size("seq")
    heads = lax.axis_size("head")
    seq = lax.axis_index("seq")
    head = lax.axis_index("head")
    tok, width = hidden_in.shape
    kv_heads, lanes = qkv_new.shape[1:]
    kv_local = kv_heads // heads
    hd = kv_cache.shape[3] // 2
    gs = lanes // hd - 2
    experts = w_gate_up.shape[0] * seqs
    capacity = max(2, tok * TOP * 5 // (4 * experts))

    def along_head(value, mask):
        pairs = [(s * heads + h, s * heads + (h ^ mask)) for s in range(seqs) for h in range(heads)]
        return lax.ppermute(value, AXES, pairs)

    def along_seq(value, mask):
        pairs = [(s * heads + h, (s ^ mask) * heads + h) for s in range(seqs) for h in range(heads)]
        return lax.ppermute(value, AXES, pairs)

    routing = jnp.concatenate([expert_ids.astype(jnp.float32), gate_weights], axis=1)
    routing = lax.all_gather(routing, AXES, tiled=True)

    by_group = qkv_new.reshape(tok, heads, kv_local, lanes).transpose(1, 2, 0, 3)
    chunks = {}
    fresh = {}
    for k in range(heads):
        part = lax.dynamic_index_in_dim(by_group, head ^ k, 0, keepdims=False)
        chunks[k], fresh[k] = part[:, :, : gs * hd], part[:, :, gs * hd :]
    order = list(range(heads - 1, 0, -1))
    for k in order:
        fresh[k] = along_head(fresh[k], k)
    for k in order:
        chunks[k] = along_head(chunks[k], k)
    fresh_rows = jnp.concatenate([fresh[k] for k in range(heads)], axis=1)
    cache = jnp.swapaxes(kv_cache[0], 0, 1)
    o_rows = o_weight.T
    arrived = []
    for k in [0] + order:
        info = jnp.stack([cache_len[0], head, head ^ k]).astype(jnp.int32)
        partial = attend(info, chunks[k], fresh_rows, cache, o_rows, tok, hd, gs)
        if k == 0:
            own = partial
        else:
            arrived.append(along_head(partial, k))
    attn_proj, normed = norm(hidden_in, norm_gain, own, jnp.stack(arrived))

    masks = [1 << b for b in range(1, seqs.bit_length() - 1)]
    orders = [masks, masks[::-1]]
    half = tok // 2

    def spread(rows):
        pieces = []
        for side, sequence in enumerate(orders):
            held = rows[side * half : (side + 1) * half]
            for mask in sequence:
                held = jnp.concatenate([held, along_seq(held, mask)], axis=0)
            pieces.append(held)
        near = jnp.concatenate(pieces, axis=0)
        return near, along_seq(near, 1)

    def offsets():
        listed = []
        for side, sequence in enumerate(orders):
            held = [0]
            for mask in sequence:
                held = held + [j ^ mask for j in held]
            listed += [(j, side) for j in held]
        return [(j, s) for j, s in listed] + [(j ^ 1, s) for j, s in listed]

    def collect(near, far):
        summed = near.astype(jnp.float32) + along_seq(far, 1).astype(jnp.float32)
        summed = summed.astype(jnp.bfloat16)
        length = near.shape[0] // 2
        pieces = []
        for side, sequence in enumerate(orders):
            held = summed[side * length : (side + 1) * length]
            for mask in sequence[::-1]:
                cut = held.shape[0] // 2
                got = along_seq(held[cut:], mask)
                held = held[:cut].astype(jnp.float32) + got.astype(jnp.float32)
                held = held.astype(jnp.bfloat16)
            pieces.append(held)
        return jnp.concatenate(pieces, axis=0)

    listed = offsets()
    block_of = jnp.array([j for j, _ in listed], jnp.int32) ^ seq
    side_of = jnp.array([s for _, s in listed], jnp.int32)
    table = routing.reshape(seqs * heads * 2, half, 2 * TOP)
    w_in = jnp.transpose(w_gate_up[0], (1, 2, 0))
    expert = seq.astype(jnp.float32).reshape(1)
    count = -(-capacity * seqs // 16) * 16
    back = []
    own_part = None
    for k in range(heads):
        rows = normed if k == 0 else along_head(normed, k)
        near, far = spread(rows)
        places = (block_of * heads + (head ^ k)) * 2 + side_of
        lists = jnp.take(table, places, axis=0).reshape(-1, 2 * TOP).T
        out_near, out_far = run_experts(
            expert, lists[:TOP], lists[TOP:], near, far, w_in, w_down[0], count
        )
        part = collect(out_near, out_far)
        if k == 0:
            own_part = part
        else:
            back.append(along_head(part, k))
    moe = own_part.astype(jnp.float32)
    for part in back:
        moe = moe + part.astype(jnp.float32)
    return attn_proj, moe.astype(jnp.bfloat16)


def solution(mesh):
    return jax.shard_map(
        per_device,
        mesh=mesh,
        in_specs=(
            P(("seq", "head"), None),
            P(("seq", "head"), None, None),
            P("seq", None, "head", None),
            P("seq"),
            P("head", None),
            P(),
            P(("seq", "head"), None),
            P(("seq", "head"), None),
            P("seq", None, None, "head"),
            P("seq", "head", None),
        ),
        out_specs=(P(("seq", "head"), None), P(("seq", "head"), None)),
        check_vma=False,
    )
```

```python
import functools

import jax
import jax.numpy as jnp
from jax import lax
from jax.experimental import pallas as pl
from jax.experimental.pallas import tpu as pltpu
from jax.sharding import PartitionSpec as P

TOP = 4
EPSILON = 1e-05
LOG2E = 1.4426950408889634
FLOOR = -1e30
AXES = ("seq", "head")
MIB = 2**20
VMEM = pltpu.VMEM
SMEM = pltpu.SMEM


def key_block(cached):
    return 2048 if cached % 2048 == 0 else cached


def attend_kernel(
    info, chunk, fresh, cache, o_weight, out, queries, acc, top, o_local, sem, *, tok, hd, gs, bk
):
    heads, cached, _ = cache.shape
    live = info[0]
    mine = info[1]
    asked = info[2]
    o_copy = pltpu.make_async_copy(o_weight, o_local, sem)
    o_copy.start()
    rows = tok * gs
    for h in range(heads):
        for r in range(gs):
            one = chunk[h, :, r * hd : (r + 1) * hd] * jnp.bfloat16(hd**-0.5)
            queries[h, r * tok : (r + 1) * tok, :] = jnp.concatenate(
                [one, jnp.zeros_like(one)], axis=1
            )
    lane = lax.broadcasted_iota(jnp.int32, (1, 2 * hd), 1)
    is_value = (lane >= hd).astype(jnp.float32).astype(jnp.bfloat16)
    is_key = (lane < hd).astype(jnp.float32).astype(jnp.bfloat16)

    def block(h, keys, mask, first):
        scores = lax.dot_general(
            queries[h], keys, (((1,), (1,)), ((), ())), preferred_element_type=jnp.float32
        )
        if mask is not None:
            scores = jnp.where(mask(scores.shape), scores, FLOOR)
        return scores

    def absorb(h, keys, scores, first):
        largest = jnp.max(scores, axis=1, keepdims=True)
        values = keys * is_value + is_key
        if first:
            now = jnp.broadcast_to(largest, top.shape[1:])
        else:
            before = top[h]
            now = jnp.maximum(before, largest)
        weights = jnp.exp2((scores - now[:, :1]) * LOG2E).astype(jnp.bfloat16)
        part = jnp.dot(weights, values, preferred_element_type=jnp.float32)
        if first:
            acc[h] = part
        else:
            acc[h] = acc[h] * jnp.exp2((before - now) * LOG2E) + part
        top[h] = now

    def causal(shape):
        column = lax.broadcasted_iota(jnp.int32, shape, 1)
        row = lax.broadcasted_iota(jnp.int32, shape, 0)
        where = (mine ^ (column // tok)) * tok + column % tok
        return where <= asked * tok + row % tok

    fresh_scores = [block(h, fresh[h], causal, True) for h in range(heads)]
    for h in range(heads):
        absorb(h, fresh[h], fresh_scores[h], True)

    def cached_step(index, masked):
        start = pl.multiple_of(index * bk, bk)
        keys = [cache[h, pl.ds(start, bk), :] for h in range(heads)]

        def alive(shape):
            return lax.broadcasted_iota(jnp.int32, shape, 1) + start < live

        scores = [block(h, keys[h], alive if masked else None, False) for h in range(heads)]
        for h in range(heads):
            absorb(h, keys[h], scores[h], False)

    full = live // bk

    def body(index, carry):
        cached_step(index, False)
        return carry

    lax.fori_loop(0, full, body, 0)

    @pl.when(full * bk < live)
    def _():
        cached_step(full, True)

    parts = []
    for h in range(heads):
        total = acc[h]
        done = (total[:, hd:] / total[:, :hd]).astype(jnp.bfloat16)
        parts += [done[r * tok : (r + 1) * tok] for r in range(gs)]
    attention = jnp.concatenate(parts, axis=1)
    o_copy.wait()
    out[...] = lax.dot_general(
        attention, o_local[...], (((1,), (1,)), ((), ())), preferred_element_type=jnp.float32
    ).astype(out.dtype)


def attend(info, chunk, fresh, cache, o_rows, tok, hd, gs):
    heads, cached, lanes = cache.shape
    width, depth = o_rows.shape
    return pl.pallas_call(
        functools.partial(attend_kernel, tok=tok, hd=hd, gs=gs, bk=key_block(cached)),
        out_shape=jax.ShapeDtypeStruct((tok, width), jnp.bfloat16),
        in_specs=[pl.BlockSpec(memory_space=SMEM)]
        + [pl.BlockSpec(memory_space=VMEM)] * 3
        + [pl.BlockSpec(memory_space=pl.ANY)],
        out_specs=pl.BlockSpec(memory_space=VMEM),
        scratch_shapes=[
            VMEM((heads, tok * gs, lanes), jnp.bfloat16),
            VMEM((heads, tok * gs, lanes), jnp.float32),
            VMEM((heads, tok * gs, 128), jnp.float32),
            VMEM((width, depth), jnp.bfloat16),
            pltpu.SemaphoreType.DMA,
        ],
        compiler_params=pltpu.CompilerParams(vmem_limit_bytes=48 * MIB),
        cost_estimate=pl.CostEstimate(
            flops=16 * heads * tok * gs * cached * hd,
            bytes_accessed=heads * cached * lanes * 2 + width * depth * 2,
            transcendentals=heads * tok * gs * cached,
        ),
        name="attend",
    )(info, chunk, fresh, cache, o_rows)


def norm_kernel(hidden, gain, ids, gates, own, others, proj, out):
    width = hidden.shape[1]
    total = own[...].astype(jnp.float32)
    for k in range(others.shape[0]):
        total = total + others[k].astype(jnp.float32)
    rounded = total.astype(jnp.bfloat16)
    proj[...] = rounded
    residual = (hidden[...].astype(jnp.float32) + rounded.astype(jnp.float32)).astype(jnp.bfloat16)
    wide = residual.astype(jnp.float32)
    mean = jnp.mean(wide * wide, axis=1, keepdims=True)
    out[:, :width] = (wide * lax.rsqrt(mean + EPSILON) * gain[...]).astype(jnp.bfloat16)
    gate = gates[...]
    high = gate.astype(jnp.bfloat16).astype(jnp.float32)
    middle = (gate - high).astype(jnp.bfloat16).astype(jnp.float32)
    low = gate - high - middle
    spare = jnp.zeros((hidden.shape[0], out.shape[1] - width - 4 * TOP), jnp.float32)
    info = jnp.concatenate([ids[...].astype(jnp.float32), high, middle, low, spare], axis=1)
    out[:, width:] = info.astype(jnp.bfloat16)


def norm(hidden, gain, ids, gates, own, others, padded):
    tok, width = hidden.shape
    return pl.pallas_call(
        norm_kernel,
        out_shape=(
            jax.ShapeDtypeStruct((tok, width), jnp.bfloat16),
            jax.ShapeDtypeStruct((tok, padded), jnp.bfloat16),
        ),
        name="norm",
        compiler_params=pltpu.CompilerParams(vmem_limit_bytes=16 * MIB),
    )(hidden, gain.reshape(1, -1), ids, gates, own, others)


def pack_kernel(*refs):
    sem = refs[-1]
    out = refs[-2]
    copies = []
    at = 0
    for i, ref in enumerate(refs[:-2]):
        length = ref.shape[0]
        copies.append(pltpu.make_async_copy(ref, out.at[pl.ds(at, length)], sem.at[i]))
        at += length
    for copy in copies:
        copy.start()
    for copy in copies:
        copy.wait()


def pack(pieces):
    total = sum(piece.shape[0] for piece in pieces)
    return pl.pallas_call(
        pack_kernel,
        out_shape=jax.ShapeDtypeStruct((total, pieces[0].shape[1]), pieces[0].dtype),
        in_specs=[pl.BlockSpec(memory_space=pl.ANY)] * len(pieces),
        out_specs=pl.BlockSpec(memory_space=pl.ANY),
        scratch_shapes=[pltpu.SemaphoreType.DMA((len(pieces),))],
        cost_estimate=pl.CostEstimate(
            flops=0, bytes_accessed=4 * total * pieces[0].shape[1], transcendentals=0
        ),
        name="pack",
    )(*pieces)


def experts_kernel(*refs, steps, extra):
    expert, near, far, w_in, w_down = refs[:5]
    out_near, out_far, rows, total, chosen, weights = refs[5 + extra :]
    step = pl.program_id(0)
    half, padded = near.shape
    width = w_down.shape[1]
    count = rows.shape[0] // 2
    segment = 256

    @pl.when(step == 0)
    def _():
        earlier = (
            lax.broadcasted_iota(jnp.int32, (segment, segment), 0)
            < lax.broadcasted_iota(jnp.int32, (segment, segment), 1)
        ).astype(jnp.float32).astype(jnp.bfloat16)
        for side, source in enumerate((near, far)):
            info = source[:, padded - 128 :].astype(jnp.float32).T
            info = info[128 - (padded - width) :]
            named = info[:TOP] == expert[0]
            picked = jnp.sum(named.astype(jnp.float32), axis=0, keepdims=True)
            gate = info[TOP : 2 * TOP] + info[2 * TOP : 3 * TOP] + info[3 * TOP : 4 * TOP]
            weight = jnp.sum(jnp.where(named, gate, 0.0), axis=0, keepdims=True)
            base = jnp.zeros((1, 1), jnp.float32)
            slots = []
            for at in range(0, half, segment):
                one = picked[:, at : at + segment]
                eight = jnp.broadcast_to(one, (16, segment)).astype(jnp.bfloat16)
                slot = jnp.dot(eight, earlier, preferred_element_type=jnp.float32)[:1]
                slots.append(slot + base)
                base = base + jnp.sum(one, axis=1, keepdims=True)
            slot = jnp.concatenate(slots, axis=1)
            slot = jnp.where(picked > 0.5, slot, -1.0).astype(jnp.int32)
            places = lax.broadcasted_iota(jnp.int32, (count, half), 0) == slot
            chosen[side] = places.astype(jnp.float32).astype(jnp.bfloat16)
            per_row = jnp.sum(jnp.where(places, weight, 0.0), axis=1, keepdims=True)
            weights[side * count : (side + 1) * count, :] = jnp.broadcast_to(
                per_row, (count, 128)
            )
            got = jnp.dot(chosen[side], source[:, :width], preferred_element_type=jnp.float32)
            rows[side * count : (side + 1) * count, :] = got.astype(jnp.bfloat16)

    contract_last = (((1,), (1,)), ((), ()))
    gate = lax.dot_general(rows[...], w_in[0], contract_last, preferred_element_type=jnp.float32)
    up = lax.dot_general(rows[...], w_in[1], contract_last, preferred_element_type=jnp.float32)
    hidden = (gate / (1.0 + jnp.exp(-gate)) * up).astype(jnp.bfloat16)
    part = jnp.dot(hidden, w_down[...], preferred_element_type=jnp.float32)

    @pl.when(step == 0)
    def _():
        total[...] = part

    @pl.when(step > 0)
    def _():
        total[...] += part

    @pl.when(step == steps - 1)
    def _():
        for side, target in enumerate((out_near, out_far)):
            here = slice(side * count, (side + 1) * count)
            scaled = (total[here, :] * weights[here, :1]).astype(jnp.bfloat16)
            target[:, :width] = lax.dot_general(
                chosen[side], scaled, (((0,), (0,)), ((), ())), preferred_element_type=jnp.float32
            ).astype(jnp.bfloat16)
            target[:, width:] = jnp.zeros((half, padded - width), jnp.bfloat16)


def run_experts(expert, near, far, w_in, w_down, count, after=()):
    half, padded = near.shape
    units, width = w_down.shape
    steps = 3 if units % 48 == 0 else 1
    part = units // steps
    whole = pl.BlockSpec((half, padded), lambda i: (0, 0), pipeline_mode=pl.Buffered(1))
    shape = jax.ShapeDtypeStruct((half, padded), jnp.bfloat16)
    return pl.pallas_call(
        functools.partial(experts_kernel, steps=steps, extra=len(after)),
        out_shape=(shape, shape),
        grid=(steps,),
        in_specs=[
            pl.BlockSpec(memory_space=SMEM),
            whole,
            whole,
            pl.BlockSpec((2, part, width), lambda i: (0, i, 0)),
            pl.BlockSpec((part, width), lambda i: (i, 0)),
        ]
        + [pl.BlockSpec(memory_space=pl.ANY)] * len(after),
        out_specs=(whole, whole),
        scratch_shapes=[
            VMEM((2 * count, width), jnp.bfloat16),
            VMEM((2 * count, width), jnp.float32),
            VMEM((2, count, half), jnp.bfloat16),
            VMEM((2 * count, 128), jnp.float32),
        ],
        compiler_params=pltpu.CompilerParams(vmem_limit_bytes=58 * MIB),
        cost_estimate=pl.CostEstimate(
            flops=4 * count * width * (units * 3 + 2 * half),
            bytes_accessed=units * width * 6 + half * padded * 8,
            transcendentals=2 * count * units,
        ),
        name="experts",
    )(expert, near, far, w_in, w_down, *after)


def plus(left, right):
    return (left.astype(jnp.float32) + right.astype(jnp.float32)).astype(jnp.bfloat16)


def fold_kernel(near, got, own, x_rows, y_rows, low, high, *, planes, tok):
    half = tok // 2
    for p in range(planes):
        for target, piece in ((own, 0), (x_rows, 1), (y_rows, 2)):
            at = (p * 4 + piece) * tok
            target[p * tok : (p + 1) * tok] = plus(near[at : at + tok], got[at : at + tok])
        at = (p * 4 + 3) * tok
        low[p * half : (p + 1) * half] = plus(near[at : at + half], got[at : at + half])
        at += half
        high[p * half : (p + 1) * half] = plus(near[at : at + half], got[at : at + half])


def fold(near, got, planes, tok):
    padded = near.shape[1]
    full = jax.ShapeDtypeStruct((planes * tok, padded), jnp.bfloat16)
    part = jax.ShapeDtypeStruct((planes * tok // 2, padded), jnp.bfloat16)
    return pl.pallas_call(
        functools.partial(fold_kernel, planes=planes, tok=tok),
        out_shape=(full, full, full, part, part),
        compiler_params=pltpu.CompilerParams(vmem_limit_bytes=32 * MIB),
        cost_estimate=pl.CostEstimate(
            flops=near.size, bytes_accessed=6 * near.size, transcendentals=0
        ),
        name="fold",
    )(near, got)


def merge_kernel(x_rows, got_low, y_rows, got_high, x_out, y_out, *, planes, tok):
    half = tok // 2
    for p in range(planes):
        a, b, c = p * tok, p * tok + half, (p + 1) * tok
        piece = slice(p * half, (p + 1) * half)
        x_out[a:b] = plus(x_rows[a:b], got_low[piece])
        x_out[b:c] = x_rows[b:c]
        y_out[a:b] = y_rows[a:b]
        y_out[b:c] = plus(y_rows[b:c], got_high[piece])


def merge(x_rows, got_low, y_rows, got_high, planes, tok):
    shape = jax.ShapeDtypeStruct(x_rows.shape, jnp.bfloat16)
    return pl.pallas_call(
        functools.partial(merge_kernel, planes=planes, tok=tok),
        out_shape=(shape, shape),
        compiler_params=pltpu.CompilerParams(vmem_limit_bytes=16 * MIB),
        cost_estimate=pl.CostEstimate(
            flops=x_rows.size, bytes_accessed=10 * x_rows.size, transcendentals=0
        ),
        name="merge",
    )(x_rows, got_low, y_rows, got_high)


def finish_kernel(own, got_x, got_y, *outs, tok):
    for p, out in enumerate(outs):
        here = slice(p * tok, (p + 1) * tok)
        total = own[here].astype(jnp.float32) + got_x[here].astype(jnp.float32)
        out[...] = (total + got_y[here].astype(jnp.float32)).astype(jnp.bfloat16)


def finish(own, got_x, got_y, planes, tok):
    shape = jax.ShapeDtypeStruct((tok, own.shape[1]), jnp.bfloat16)
    return pl.pallas_call(
        functools.partial(finish_kernel, tok=tok),
        out_shape=(shape,) * planes,
        compiler_params=pltpu.CompilerParams(vmem_limit_bytes=16 * MIB),
        cost_estimate=pl.CostEstimate(
            flops=own.size, bytes_accessed=8 * own.size, transcendentals=0
        ),
        name="finish",
    )(own, got_x, got_y)


def last_kernel(own, first, second, out):
    width = out.shape[1]
    total = own[:, :width].astype(jnp.float32) + first[:, :width].astype(jnp.float32)
    out[...] = (total + second[:, :width].astype(jnp.float32)).astype(jnp.bfloat16)


def per_device(
    hidden_in, qkv_new, kv_cache, cache_len, o_weight, norm_gain,
    expert_ids, gate_weights, w_gate_up, w_down,
):
    seqs = lax.axis_size("seq")
    heads = lax.axis_size("head")
    seq = lax.axis_index("seq")
    head = lax.axis_index("head")
    tok, width = hidden_in.shape
    kv_heads, lanes = qkv_new.shape[1:]
    kv_local = kv_heads // heads
    hd = kv_cache.shape[3] // 2
    gs = lanes // hd - 2
    experts = w_gate_up.shape[0] * seqs
    capacity = max(2, tok * TOP * 5 // (4 * experts))
    padded = -(-(width + 4 * TOP) // 128) * 128

    def along_head(value, mask):
        pairs = [(s * heads + h, s * heads + (h ^ mask)) for s in range(seqs) for h in range(heads)]
        return lax.ppermute(value, AXES, pairs)

    def along_seq(value, mask):
        pairs = [(s * heads + h, (s ^ mask) * heads + h) for s in range(seqs) for h in range(heads)]
        return lax.ppermute(value, AXES, pairs)

    by_group = qkv_new.reshape(tok, heads, kv_local, lanes).transpose(1, 2, 0, 3)
    chunks = {}
    fresh = {}
    for k in range(heads):
        part = lax.dynamic_index_in_dim(by_group, head ^ k, 0, keepdims=False)
        chunks[k], fresh[k] = part[:, :, : gs * hd], part[:, :, gs * hd :]
    order = list(range(heads - 1, 0, -1))
    for k in order:
        fresh[k] = along_head(fresh[k], k)
    for k in order:
        chunks[k] = along_head(chunks[k], k)
    fresh_rows = jnp.concatenate([fresh[k] for k in range(heads)], axis=1)
    cache = jnp.swapaxes(kv_cache[0], 0, 1)
    o_rows = o_weight.T
    arrived = []
    for k in [0] + order:
        info = jnp.stack([cache_len[0], head, head ^ k]).astype(jnp.int32)
        partial = attend(info, chunks[k], fresh_rows, cache, o_rows, tok, hd, gs)
        if k == 0:
            own = partial
        else:
            arrived.append(along_head(partial, k))
    attn_proj, rows = norm(
        hidden_in, norm_gain, expert_ids, gate_weights, own, jnp.stack(arrived), padded
    )

    w_in = jnp.transpose(w_gate_up[0], (1, 2, 0))
    expert = seq.astype(jnp.float32).reshape(1)
    plane = {0: rows, 1: along_head(rows, 1), 2: along_head(rows, 2)}
    plane[3] = along_head(plane[2], 1)

    if seqs == 8:
        half = tok // 2
        count = -(-capacity * seqs // 16) * 16

        def spread(own_rows):
            by_x = along_seq(own_rows, 2)
            by_y = along_seq(own_rows, 4)
            low = along_seq(by_x[:half], 4)
            high = along_seq(by_y[half:], 2)
            return [own_rows, by_x, by_y, low, high]

        def collect(near, far):
            own_rows, x_rows, y_rows, low, high = fold(near, along_seq(far, 1), 2, tok)
            got_low = along_seq(low, 4)
            got_high = along_seq(high, 2)
            x_rows, y_rows = merge(x_rows, got_low, y_rows, got_high, 2, tok)
            return own_rows, x_rows, y_rows

        pieces = {k: spread(plane[k]) for k in range(4)}
        near0 = pack(pieces[0] + pieces[1])
        far0 = along_seq(near0, 1)
        near1 = pack(pieces[2] + pieces[3])
        far1 = along_seq(near1, 1)
        back0 = run_experts(expert, near0, far0, w_in, w_down[0], count, (plane[3],))
        kept0 = collect(*back0)
        back1 = run_experts(expert, near1, far1, w_in, w_down[0], count, (kept0[0],))
        kept1 = collect(*back1)
        done = []
        for own_rows, x_rows, y_rows in (kept0, kept1):
            done += finish(own_rows, along_seq(x_rows, 2), along_seq(y_rows, 4), 2, tok)
    else:
        masks = [1 << b for b in range(1, seqs.bit_length() - 1)]
        count = -(-capacity * (seqs // 2) // 16) * 16
        done = []
        for k in range(4):
            near = plane[k]
            for mask in masks:
                near = jnp.concatenate([near, along_seq(near, mask)], axis=0)
            far = along_seq(near, 1)
            near, far = run_experts(expert, near, far, w_in, w_down[0], count)
            near = plus(near, along_seq(far, 1))
            for mask in masks[::-1]:
                cut = near.shape[0] // 2
                near = plus(near[:cut], along_seq(near[cut:], mask))
            done.append(near)
    first = along_head(done[1], 1)
    pair = plus(done[2], along_head(done[3], 1))
    second = along_head(pair, 2)
    moe = pl.pallas_call(
        last_kernel, out_shape=jax.ShapeDtypeStruct((tok, width), jnp.bfloat16), name="last"
    )(done[0], first, second)
    return attn_proj, moe


def solution(mesh):
    return jax.shard_map(
        per_device,
        mesh=mesh,
        in_specs=(
            P(("seq", "head"), None),
            P(("seq", "head"), None, None),
            P("seq", None, "head", None),
            P("seq"),
            P("head", None),
            P(),
            P(("seq", "head"), None),
            P(("seq", "head"), None),
            P("seq", None, None, "head"),
            P("seq", "head", None),
        ),
        out_specs=(P(("seq", "head"), None), P(("seq", "head"), None)),
        check_vma=False,
    )
```

```python
import functools

import jax
import jax.numpy as jnp
from jax import lax
from jax.experimental import pallas as pl
from jax.experimental.pallas import tpu as pltpu
from jax.sharding import PartitionSpec as P

TOP = 4
EPSILON = 1e-05
LOG2E = 1.4426950408889634
FLOOR = -1e30
AXES = ("seq", "head")
MIB = 2**20
VMEM = pltpu.VMEM
LONG = pl.CostEstimate(flops=2 * 10**10, bytes_accessed=10**8, transcendentals=0)
SHORT = pl.CostEstimate(flops=1, bytes_accessed=1, transcendentals=0)
SMEM = pltpu.SMEM


def key_block(cached):
    return 2048 if cached % 2048 == 0 else cached


def attend_kernel(
    info, chunk, fresh, cache_far, o_weight, out, queries, acc, top, cache, o_local, sems,
    *, tok, hd, gs, bk
):
    heads, cached, _ = cache_far.shape
    live = info[0]
    mine = info[1]
    asked = info[2]
    blocks = cached // bk

    def cache_copy(index):
        here = pl.ds(pl.multiple_of(index * bk, bk), bk)
        return pltpu.make_async_copy(cache_far.at[:, here], cache.at[:, here], sems.at[index])

    def begin(index, carry):
        cache_copy(index).start()
        return carry

    used = (live + bk - 1) // bk
    lax.fori_loop(0, used, begin, 0)
    o_copy = pltpu.make_async_copy(o_weight, o_local, sems.at[blocks])
    o_copy.start()
    rows = tok * gs
    for h in range(heads):
        for r in range(gs):
            one = chunk[h, :, r * hd : (r + 1) * hd] * jnp.bfloat16(hd**-0.5)
            queries[h, r * tok : (r + 1) * tok, :] = jnp.concatenate(
                [one, jnp.zeros_like(one)], axis=1
            )
    lane = lax.broadcasted_iota(jnp.int32, (1, 2 * hd), 1)
    is_value = (lane >= hd).astype(jnp.float32).astype(jnp.bfloat16)
    is_key = (lane < hd).astype(jnp.float32).astype(jnp.bfloat16)

    def block(h, keys, mask, first):
        scores = lax.dot_general(
            queries[h], keys, (((1,), (1,)), ((), ())), preferred_element_type=jnp.float32
        )
        if mask is not None:
            scores = jnp.where(mask(scores.shape), scores, FLOOR)
        return scores

    def absorb(h, keys, scores, first):
        largest = jnp.max(scores, axis=1, keepdims=True)
        values = keys * is_value + is_key
        if first:
            now = jnp.broadcast_to(largest, top.shape[1:])
        else:
            before = top[h]
            now = jnp.maximum(before, largest)
        weights = jnp.exp2((scores - now[:, :1]) * LOG2E).astype(jnp.bfloat16)
        part = jnp.dot(weights, values, preferred_element_type=jnp.float32)
        if first:
            acc[h] = part
        else:
            acc[h] = acc[h] * jnp.exp2((before - now) * LOG2E) + part
        top[h] = now

    def causal(shape):
        column = lax.broadcasted_iota(jnp.int32, shape, 1)
        row = lax.broadcasted_iota(jnp.int32, shape, 0)
        where = (mine ^ (column // tok)) * tok + column % tok
        return where <= asked * tok + row % tok

    fresh_scores = [block(h, fresh[h], causal, True) for h in range(heads)]
    for h in range(heads):
        absorb(h, fresh[h], fresh_scores[h], True)

    def cached_step(index, masked):
        start = pl.multiple_of(index * bk, bk)
        cache_copy(index).wait()
        keys = [cache[h, pl.ds(start, bk), :] for h in range(heads)]

        def alive(shape):
            return lax.broadcasted_iota(jnp.int32, shape, 1) + start < live

        scores = [block(h, keys[h], alive if masked else None, False) for h in range(heads)]
        for h in range(heads):
            absorb(h, keys[h], scores[h], False)

    full = live // bk

    def body(index, carry):
        cached_step(index, False)
        return carry

    lax.fori_loop(0, full, body, 0)

    @pl.when(full * bk < live)
    def _():
        cached_step(full, True)

    parts = []
    for h in range(heads):
        total = acc[h]
        done = (total[:, hd:] / total[:, :hd]).astype(jnp.bfloat16)
        parts += [done[r * tok : (r + 1) * tok] for r in range(gs)]
    attention = jnp.concatenate(parts, axis=1)
    o_copy.wait()
    out[...] = lax.dot_general(
        attention, o_local[...], (((1,), (1,)), ((), ())), preferred_element_type=jnp.float32
    ).astype(out.dtype)


def attend(info, chunk, fresh, cache, o_rows, tok, hd, gs):
    heads, cached, lanes = cache.shape
    width, depth = o_rows.shape
    return pl.pallas_call(
        functools.partial(attend_kernel, tok=tok, hd=hd, gs=gs, bk=key_block(cached)),
        out_shape=jax.ShapeDtypeStruct((tok, width), jnp.bfloat16),
        in_specs=[pl.BlockSpec(memory_space=SMEM)]
        + [pl.BlockSpec(memory_space=VMEM)] * 2
        + [pl.BlockSpec(memory_space=pl.ANY)] * 2,
        out_specs=pl.BlockSpec(memory_space=VMEM),
        scratch_shapes=[
            VMEM((heads, tok * gs, lanes), jnp.bfloat16),
            VMEM((heads, tok * gs, lanes), jnp.float32),
            VMEM((heads, tok * gs, 128), jnp.float32),
            VMEM(cache.shape, jnp.bfloat16),
            VMEM((width, depth), jnp.bfloat16),
            pltpu.SemaphoreType.DMA((cached // key_block(cached) + 1,)),
        ],
        compiler_params=pltpu.CompilerParams(vmem_limit_bytes=48 * MIB),
        cost_estimate=SHORT,
        name="attend",
    )(info, chunk, fresh, cache, o_rows)


def norm_kernel(hidden, gain, ids, gates, own, others, proj, out):
    width = hidden.shape[1]
    total = own[...].astype(jnp.float32)
    for k in range(others.shape[0]):
        total = total + others[k].astype(jnp.float32)
    rounded = total.astype(jnp.bfloat16)
    proj[...] = rounded
    residual = (hidden[...].astype(jnp.float32) + rounded.astype(jnp.float32)).astype(jnp.bfloat16)
    wide = residual.astype(jnp.float32)
    mean = jnp.mean(wide * wide, axis=1, keepdims=True)
    out[:, :width] = (wide * lax.rsqrt(mean + EPSILON) * gain[...]).astype(jnp.bfloat16)
    gate = gates[...]
    high = gate.astype(jnp.bfloat16).astype(jnp.float32)
    middle = (gate - high).astype(jnp.bfloat16).astype(jnp.float32)
    low = gate - high - middle
    spare = jnp.zeros((hidden.shape[0], out.shape[1] - width - 4 * TOP), jnp.float32)
    info = jnp.concatenate([ids[...].astype(jnp.float32), high, middle, low, spare], axis=1)
    out[:, width:] = info.astype(jnp.bfloat16)


def norm(hidden, gain, ids, gates, own, others, padded):
    tok, width = hidden.shape
    return pl.pallas_call(
        norm_kernel,
        out_shape=(
            jax.ShapeDtypeStruct((tok, width), jnp.bfloat16),
            jax.ShapeDtypeStruct((tok, padded), jnp.bfloat16),
        ),
        name="norm",
        compiler_params=pltpu.CompilerParams(vmem_limit_bytes=16 * MIB),
    )(hidden, gain.reshape(1, -1), ids, gates, own, others)


TOKEN = jax.ShapeDtypeStruct((8, 128), jnp.float32)


def small(kernel, name, inputs, shapes, after):
    given = len(inputs)

    def body(*refs):
        kernel(*refs[:given], *refs[given + len(after) : -1])
        refs[-1][...] = jnp.zeros_like(refs[-1])

    moved = sum(x.size for x in inputs) + sum(x.size for x in shapes)
    return pl.pallas_call(
        body,
        out_shape=tuple(shapes) + (TOKEN,),
        in_specs=[pl.BlockSpec(memory_space=VMEM)] * given
        + [pl.BlockSpec(memory_space=pl.ANY)] * len(after),
        out_specs=tuple([pl.BlockSpec(memory_space=VMEM)] * (len(shapes) + 1)),
        compiler_params=pltpu.CompilerParams(vmem_limit_bytes=16 * MIB),
        cost_estimate=LONG,
        name=name,
    )(*inputs, *after)


def rows_like(rows, value):
    return jax.ShapeDtypeStruct((rows, value.shape[1]), value.dtype)


def assemble_kernel(*refs, plan):
    outs = refs[len(refs) - len(plan) :]
    for out, pieces in zip(outs, plan):
        at = 0
        for length, terms in pieces:
            first, start = terms[0]
            total = refs[first][start : start + length]
            if len(terms) > 1:
                total = total.astype(jnp.float32)
                for source, start in terms[1:]:
                    total = total + refs[source][start : start + length].astype(jnp.float32)
            out[at : at + length] = total.astype(out.dtype)
            at += length


def assemble(name, arrays, results, after):
    used = []
    plan = []
    for pieces in results:
        listed = []
        for length, terms in pieces:
            for key, _ in terms:
                if key not in used:
                    used.append(key)
            listed.append((length, tuple((used.index(key), start) for key, start in terms)))
        plan.append(listed)
    inputs = [arrays[key] for key in used]
    shapes = [rows_like(sum(length for length, _ in pieces), inputs[0]) for pieces in plan]
    return small(functools.partial(assemble_kernel, plan=plan), name, inputs, shapes, after)


def experts_kernel(*refs, steps, extra):
    expert, near, far, w_in, w_down = refs[:5]
    out_near, out_far, token, rows, total, chosen, weights = refs[5 + extra :]
    step = pl.program_id(0)
    half, padded = near.shape
    width = w_down.shape[1]
    count = rows.shape[0] // 2
    segment = 256

    @pl.when(step == 0)
    def _():
        earlier = (
            lax.broadcasted_iota(jnp.int32, (segment, segment), 0)
            < lax.broadcasted_iota(jnp.int32, (segment, segment), 1)
        ).astype(jnp.float32).astype(jnp.bfloat16)
        for side, source in enumerate((near, far)):
            info = source[:, padded - 128 :].astype(jnp.float32).T
            info = info[128 - (padded - width) :]
            named = info[:TOP] == expert[0]
            picked = jnp.sum(named.astype(jnp.float32), axis=0, keepdims=True)
            gate = info[TOP : 2 * TOP] + info[2 * TOP : 3 * TOP] + info[3 * TOP : 4 * TOP]
            weight = jnp.sum(jnp.where(named, gate, 0.0), axis=0, keepdims=True)
            base = jnp.zeros((1, 1), jnp.float32)
            slots = []
            for at in range(0, half, segment):
                one = picked[:, at : at + segment]
                eight = jnp.broadcast_to(one, (16, segment)).astype(jnp.bfloat16)
                slot = jnp.dot(eight, earlier, preferred_element_type=jnp.float32)[:1]
                slots.append(slot + base)
                base = base + jnp.sum(one, axis=1, keepdims=True)
            slot = jnp.concatenate(slots, axis=1)
            slot = jnp.where(picked > 0.5, slot, -1.0).astype(jnp.int32)
            places = lax.broadcasted_iota(jnp.int32, (count, half), 0) == slot
            chosen[side] = places.astype(jnp.float32).astype(jnp.bfloat16)
            per_row = jnp.sum(jnp.where(places, weight, 0.0), axis=1, keepdims=True)
            weights[side * count : (side + 1) * count, :] = jnp.broadcast_to(
                per_row, (count, 128)
            )
            got = jnp.dot(chosen[side], source[:, :width], preferred_element_type=jnp.float32)
            rows[side * count : (side + 1) * count, :] = got.astype(jnp.bfloat16)

    contract_last = (((1,), (1,)), ((), ()))
    gate = lax.dot_general(rows[...], w_in[0], contract_last, preferred_element_type=jnp.float32)
    up = lax.dot_general(rows[...], w_in[1], contract_last, preferred_element_type=jnp.float32)
    hidden = (gate / (1.0 + jnp.exp(-gate)) * up).astype(jnp.bfloat16)
    part = jnp.dot(hidden, w_down[...], preferred_element_type=jnp.float32)

    @pl.when(step == 0)
    def _():
        total[...] = part

    @pl.when(step > 0)
    def _():
        total[...] += part

    @pl.when(step == steps - 1)
    def _():
        token[...] = jnp.zeros_like(token)
        for side, target in enumerate((out_near, out_far)):
            here = slice(side * count, (side + 1) * count)
            scaled = (total[here, :] * weights[here, :1]).astype(jnp.bfloat16)
            target[:, :width] = lax.dot_general(
                chosen[side], scaled, (((0,), (0,)), ((), ())), preferred_element_type=jnp.float32
            ).astype(jnp.bfloat16)
            target[:, width:] = jnp.zeros((half, padded - width), jnp.bfloat16)


def run_experts(expert, near, far, w_in, w_down, count, after=()):
    half, padded = near.shape
    units, width = w_down.shape
    steps = 3 if units % 48 == 0 else 1
    part = units // steps
    whole = pl.BlockSpec((half, padded), lambda i: (0, 0), pipeline_mode=pl.Buffered(1))
    shape = jax.ShapeDtypeStruct((half, padded), jnp.bfloat16)
    return pl.pallas_call(
        functools.partial(experts_kernel, steps=steps, extra=len(after)),
        out_shape=(shape, shape, TOKEN),
        grid=(steps,),
        in_specs=[
            pl.BlockSpec(memory_space=SMEM),
            whole,
            whole,
            pl.BlockSpec((2, part, width), lambda i: (0, i, 0)),
            pl.BlockSpec((part, width), lambda i: (i, 0)),
        ]
        + [pl.BlockSpec(memory_space=pl.ANY)] * len(after),
        out_specs=(whole, whole, pl.BlockSpec(TOKEN.shape, lambda i: (0, 0))),
        scratch_shapes=[
            VMEM((2 * count, width), jnp.bfloat16),
            VMEM((2 * count, width), jnp.float32),
            VMEM((2, count, half), jnp.bfloat16),
            VMEM((2 * count, 128), jnp.float32),
        ],
        compiler_params=pltpu.CompilerParams(vmem_limit_bytes=(58 if half > 256 else 32) * MIB),
        cost_estimate=SHORT,
        name="experts",
    )(expert, near, far, w_in, w_down, *after)


def plus(left, right):
    return (left.astype(jnp.float32) + right.astype(jnp.float32)).astype(jnp.bfloat16)


def last_kernel(*refs):
    out = refs[-1]
    width = out.shape[1]
    total = refs[0][:, :width].astype(jnp.float32)
    for ref in refs[1:-1]:
        total = total + ref[:, :width].astype(jnp.float32)
    out[...] = total.astype(jnp.bfloat16)


def per_device(
    hidden_in, qkv_new, kv_cache, cache_len, o_weight, norm_gain,
    expert_ids, gate_weights, w_gate_up, w_down,
):
    seqs = lax.axis_size("seq")
    heads = lax.axis_size("head")
    seq = lax.axis_index("seq")
    head = lax.axis_index("head")
    tok, width = hidden_in.shape
    kv_heads, lanes = qkv_new.shape[1:]
    kv_local = kv_heads // heads
    hd = kv_cache.shape[3] // 2
    gs = lanes // hd - 2
    experts = w_gate_up.shape[0] * seqs
    capacity = max(2, tok * TOP * 5 // (4 * experts))
    padded = -(-(width + 4 * TOP) // 128) * 128

    def along_head(value, mask):
        pairs = [(s * heads + h, s * heads + (h ^ mask)) for s in range(seqs) for h in range(heads)]
        return lax.ppermute(value, AXES, pairs)

    def along_seq(value, mask):
        pairs = [(s * heads + h, (s ^ mask) * heads + h) for s in range(seqs) for h in range(heads)]
        return lax.ppermute(value, AXES, pairs)

    by_group = qkv_new.reshape(tok, heads, kv_local, lanes).transpose(1, 2, 0, 3)
    chunks = {}
    fresh = {}
    for k in range(heads):
        part = lax.dynamic_index_in_dim(by_group, head ^ k, 0, keepdims=False)
        chunks[k], fresh[k] = part[:, :, : gs * hd], part[:, :, gs * hd :]
    order = list(range(heads - 1, 0, -1))
    for k in order:
        fresh[k] = along_head(fresh[k], k)
    for k in order:
        chunks[k] = along_head(chunks[k], k)
    fresh_rows = jnp.concatenate([fresh[k] for k in range(heads)], axis=1)
    cache = jnp.swapaxes(kv_cache[0], 0, 1)
    o_rows = o_weight.T
    arrived = []
    for k in [0] + order:
        info = jnp.stack([cache_len[0], head, head ^ k]).astype(jnp.int32)
        partial = attend(info, chunks[k], fresh_rows, cache, o_rows, tok, hd, gs)
        if k == 0:
            own = partial
        else:
            arrived.append(along_head(partial, k))
    attn_proj, rows = norm(
        hidden_in, norm_gain, expert_ids, gate_weights, own, jnp.stack(arrived), padded
    )

    w_in = jnp.transpose(w_gate_up[0], (1, 2, 0))
    expert = seq.astype(jnp.float32).reshape(1)
    plane = {0: rows, 1: along_head(rows, 1), 2: along_head(rows, 2)}
    plane[3] = along_head(plane[2], 1)

    if seqs == 8:
        count = -(-capacity * (seqs // 2) // 16) * 16
        half = tok // 2
        x_at, y_at, low_at, high_at = tok, 2 * tok, 3 * tok, 3 * tok + half
        got = {f"p{k}": plane[k] for k in range(4)}
        done = []
        latest = [jnp.zeros(TOKEN.shape, TOKEN.dtype)]

        def exchange(stage, to_x, to_y):
            got[f"x{stage}"] = along_seq(to_x, 2)
            got[f"y{stage}"] = along_seq(to_y, 4)

        def run(name, results):
            *made, latest[0] = assemble(name, got, results, latest)
            return made

        def experts_of(k):
            got[f"b{k}"], sent, latest[0] = run_experts(
                expert, got[f"n{k}"], far[k], w_in, w_down[0], count, latest
            )
            got[f"r{k}"] = along_seq(sent, 1)

        def summed(k, start, length, *more):
            return (length, [(f"b{k}", start), (f"r{k}", start), *more])

        def near_of(k, stage, at):
            return [
                (tok, [(f"p{k}", 0)]), (tok, [(f"x{k}", 0)]), (tok, [(f"y{k}", 0)]),
                (half, [(f"y{stage}", at)]), (half, [(f"x{stage}", at)]),
            ]

        def returned(k, stage, at):
            return (
                [summed(k, x_at, half, (f"y{stage}", at)), summed(k, x_at + half, half)],
                [summed(k, y_at, half), summed(k, y_at + half, half, (f"x{stage}", at))],
            )

        far = {}
        exchange(0, rows, rows)
        for stage in range(1, 4):
            results = [
                [(tok, [(f"p{stage}", 0)]), (half, [(f"y{stage - 1}", half)])],
                [(tok, [(f"p{stage}", 0)]), (half, [(f"x{stage - 1}", 0)])],
            ]
            if stage > 1:
                results.append(near_of(stage - 2, stage - 1, tok))
            made = run("gather", results)
            exchange(stage, made[0], made[1])
            if stage > 1:
                got[f"n{stage - 2}"] = made[2]
                far[stage - 2] = along_seq(made[2], 1)
                experts_of(stage - 2)
        made = run("turn", [
            [(half, [("y3", half)]), summed(0, high_at, half)],
            [(half, [("x3", 0)]), summed(0, low_at, half)],
            near_of(2, 3, tok),
        ])
        exchange(4, made[0], made[1])
        got["n2"] = made[2]
        far[2] = along_seq(made[2], 1)
        experts_of(2)
        to_x, to_y = returned(0, 4, half)
        made = run("turn", [
            to_x + [summed(1, high_at, half)],
            to_y + [summed(1, low_at, half)],
            near_of(3, 4, 0),
        ])
        exchange(5, made[0], made[1])
        got["n3"] = made[2]
        far[3] = along_seq(made[2], 1)
        got["h2"], got["l2"] = run(
            "ahead", [[summed(2, high_at, half)], [summed(2, low_at, half)]]
        )
        experts_of(3)
        for k in range(4):
            stage = 5 + k
            finished = [summed(k, 0, tok, (f"x{stage}", 0), (f"y{stage}", 0))]
            if k == 3:
                done += run("reduce", [finished])
                break
            to_x, to_y = returned(k + 1, stage, tok)
            if k == 0:
                to_x = to_x + [(half, [("h2", 0)])]
                to_y = to_y + [(half, [("l2", 0)])]
            if k == 1:
                to_x = to_x + [summed(3, high_at, half)]
                to_y = to_y + [summed(3, low_at, half)]
            made = run("reduce", [to_x, to_y, finished])
            exchange(stage + 1, made[0], made[1])
            done.append(made[2])
    else:
        masks = [1 << b for b in range(1, seqs.bit_length() - 1)]
        count = -(-capacity * (seqs // 2) // 16) * 16
        done = []
        for k in range(4):
            near = plane[k]
            for mask in masks:
                near = jnp.concatenate([near, along_seq(near, mask)], axis=0)
            far = along_seq(near, 1)
            near, far, _ = run_experts(expert, near, far, w_in, w_down[0], count)
            near = plus(near, along_seq(far, 1))
            for mask in masks[::-1]:
                cut = near.shape[0] // 2
                near = plus(near[:cut], along_seq(near[cut:], mask))
            done.append(near)
    others = [along_head(done[k], k) for k in range(1, heads)]
    moe = pl.pallas_call(
        last_kernel, out_shape=jax.ShapeDtypeStruct((tok, width), jnp.bfloat16), name="last"
    )(done[0], *others)
    return attn_proj, moe


def solution(mesh):
    return jax.shard_map(
        per_device,
        mesh=mesh,
        in_specs=(
            P(("seq", "head"), None),
            P(("seq", "head"), None, None),
            P("seq", None, "head", None),
            P("seq"),
            P("head", None),
            P(),
            P(("seq", "head"), None),
            P(("seq", "head"), None),
            P("seq", None, None, "head"),
            P("seq", "head", None),
        ),
        out_specs=(P(("seq", "head"), None), P(("seq", "head"), None)),
        check_vma=False,
    )
```

```python
import functools

import jax
import jax.numpy as jnp
from jax import lax
from jax.experimental import pallas as pl
from jax.experimental.pallas import tpu as pltpu
from jax.sharding import PartitionSpec as P

TOP = 4
EPSILON = 1e-05
LOG2E = 1.4426950408889634
FLOOR = -1e30
AXES = ("seq", "head")
MIB = 2**20
TOKEN = jax.ShapeDtypeStruct((8, 128), jnp.float32)
VMEM = pltpu.VMEM
LONG = pl.CostEstimate(flops=2 * 10**10, bytes_accessed=10**8, transcendentals=0)
SHORT = pl.CostEstimate(flops=1, bytes_accessed=1, transcendentals=0)
SMEM = pltpu.SMEM


def key_block(cached):
    return 2048 if cached % 2048 == 0 else cached


def attend_kernel(*refs, tok, hd, gs, bk, cached, mode):
    refs = list(refs)
    if mode != "start":
        refs.pop(0)
    info = refs.pop(0)
    chunk = refs.pop(0)
    cache_far = refs.pop(0)
    if mode != "start":
        parts = [refs.pop(0) for _ in range(4)]
        o_weight = refs.pop(0)
    if mode == "end":
        acc_in, top_in = refs.pop(0), refs.pop(0)
    if mode == "start":
        acc, top, token = refs.pop(0), refs.pop(0), refs.pop(0)
        queries, cache, sems = refs
    else:
        out, token = refs.pop(0), refs.pop(0)
        acc, top, queries, cache, o_local, sems = refs
    token[...] = jnp.zeros_like(token)
    heads = cache.shape[0]
    blocks = cached // bk
    live, mine, asked = info[0], info[1], info[2]
    last = (live - 1) // bk

    def cache_copy(index):
        here = pl.ds(pl.multiple_of(index * bk, bk), bk)
        return pltpu.make_async_copy(cache_far.at[:, here], cache.at[:, here], sems.at[index])

    def begin(index, carry):
        cache_copy(index).start()
        return carry

    first_block = last if mode == "end" else 0
    lax.fori_loop(first_block, last if mode == "start" else last + 1, begin, 0)
    if mode != "start":
        o_copy = pltpu.make_async_copy(o_weight, o_local, sems.at[blocks])
        o_copy.start()
    for h in range(heads):
        for r in range(gs):
            one = chunk[h, :, r * hd : (r + 1) * hd] * jnp.bfloat16(hd**-0.5)
            queries[h, r * tok : (r + 1) * tok, :] = jnp.concatenate(
                [one, jnp.zeros_like(one)], axis=1
            )
    lane = lax.broadcasted_iota(jnp.int32, (1, 2 * hd), 1)
    is_value = (lane >= hd).astype(jnp.float32).astype(jnp.bfloat16)
    is_key = (lane < hd).astype(jnp.float32).astype(jnp.bfloat16)
    if mode == "end":
        acc[...] = acc_in[...]
        top[...] = top_in[...]
    elif mode == "start":
        acc[...] = jnp.zeros_like(acc)
        top[...] = jnp.full_like(top, FLOOR)

    def block(h, keys, mask):
        scores = lax.dot_general(
            queries[h], keys, (((1,), (1,)), ((), ())), preferred_element_type=jnp.float32
        )
        if mask is not None:
            scores = jnp.where(mask(scores.shape), scores, FLOOR)
        return scores

    def absorb(h, keys, scores, empty=False):
        values = keys * is_value + is_key
        largest = jnp.max(scores, axis=1, keepdims=True)
        if empty:
            now = jnp.broadcast_to(largest, top.shape[1:])
        else:
            before = top[h]
            now = jnp.maximum(before, largest)
        weights = jnp.exp2((scores - now[:, :1]) * LOG2E).astype(jnp.bfloat16)
        part = jnp.dot(weights, values, preferred_element_type=jnp.float32)
        acc[h] = part if empty else acc[h] * jnp.exp2((before - now) * LOG2E) + part
        top[h] = now

    def causal(shape):
        column = lax.broadcasted_iota(jnp.int32, shape, 1)
        row = lax.broadcasted_iota(jnp.int32, shape, 0)
        where = (mine ^ (column // tok)) * tok + column % tok
        return where <= asked * tok + row % tok

    def new_keys():
        fresh = [
            jnp.concatenate([part[h, :, gs * hd :] for part in parts], axis=0)
            for h in range(heads)
        ]
        scores = [block(h, fresh[h], causal) for h in range(heads)]
        for h in range(heads):
            absorb(h, fresh[h], scores[h], mode == "whole")

    def cached_step(index, masked):
        start = pl.multiple_of(index * bk, bk)
        cache_copy(index).wait()
        keys = [cache[h, pl.ds(start, bk), :] for h in range(heads)]

        def alive(shape):
            return lax.broadcasted_iota(jnp.int32, shape, 1) + start < live

        scores = [block(h, keys[h], alive if masked else None) for h in range(heads)]
        for h in range(heads):
            absorb(h, keys[h], scores[h])

    def body(index, carry):
        cached_step(index, False)
        return carry

    if mode != "start":
        new_keys()
    full = last if mode == "start" else live // bk
    lax.fori_loop(first_block, full, body, 0)
    if mode == "start":
        return

    @pl.when(full * bk < live)
    def _():
        cached_step(full, True)

    pieces = []
    for h in range(heads):
        total = acc[h]
        done = (total[:, hd:] / total[:, :hd]).astype(jnp.bfloat16)
        pieces += [done[r * tok : (r + 1) * tok] for r in range(gs)]
    attention = jnp.concatenate(pieces, axis=1)
    o_copy.wait()
    out[...] = lax.dot_general(
        attention, o_local[...], (((1,), (1,)), ((), ())), preferred_element_type=jnp.float32
    ).astype(out.dtype)


def attend(mode, after, info, chunk, cache, parts, o_rows, state, tok, hd, gs):
    heads, cached, lanes = cache.shape
    width, depth = o_rows.shape
    bk = key_block(cached)
    vmem = pl.BlockSpec(memory_space=VMEM)
    anywhere = pl.BlockSpec(memory_space=pl.ANY)
    inputs, specs = [info, chunk, cache], [pl.BlockSpec(memory_space=SMEM), vmem, anywhere]
    if mode != "start":
        inputs += [*parts, o_rows]
        specs += [vmem] * 4 + [anywhere]
    if mode == "end":
        inputs += list(state)
        specs += [vmem] * 2
    if mode != "start":
        inputs, specs = [after] + inputs, [anywhere] + specs
    held = (heads, tok * gs, lanes)
    state_shape = jax.ShapeDtypeStruct(held, jnp.float32)
    scratch = [
        VMEM(held, jnp.bfloat16),
        VMEM(cache.shape, jnp.bfloat16),
        pltpu.SemaphoreType.DMA((cached // bk + 1,)),
    ]
    if mode != "start":
        scratch = [VMEM(held, jnp.float32)] * 2 + scratch
        scratch.insert(4, VMEM((width, depth), jnp.bfloat16))
    return pl.pallas_call(
        functools.partial(
            attend_kernel, tok=tok, hd=hd, gs=gs, bk=bk, cached=cached, mode=mode
        ),
        out_shape=(state_shape, state_shape, TOKEN)
        if mode == "start"
        else (jax.ShapeDtypeStruct((tok, width), jnp.bfloat16), TOKEN),
        in_specs=specs,
        out_specs=(vmem,) * (3 if mode == "start" else 2),
        scratch_shapes=scratch,
        compiler_params=pltpu.CompilerParams(vmem_limit_bytes=48 * MIB),
        cost_estimate=SHORT,
        name="attend_" + mode,
    )(*inputs)


def norm_kernel(hidden, gain, ids, gates, own, *refs):
    *others, proj, out = refs
    width = hidden.shape[1]
    total = own[...].astype(jnp.float32)
    for other in others:
        total = total + other[...].astype(jnp.float32)
    rounded = total.astype(jnp.bfloat16)
    proj[...] = rounded
    residual = (hidden[...].astype(jnp.float32) + rounded.astype(jnp.float32)).astype(jnp.bfloat16)
    wide = residual.astype(jnp.float32)
    mean = jnp.mean(wide * wide, axis=1, keepdims=True)
    out[:, :width] = (wide * lax.rsqrt(mean + EPSILON) * gain[...]).astype(jnp.bfloat16)
    gate = gates[...]
    high = gate.astype(jnp.bfloat16).astype(jnp.float32)
    middle = (gate - high).astype(jnp.bfloat16).astype(jnp.float32)
    low = gate - high - middle
    spare = jnp.zeros((hidden.shape[0], out.shape[1] - width - 4 * TOP), jnp.float32)
    info = jnp.concatenate([ids[...].astype(jnp.float32), high, middle, low, spare], axis=1)
    out[:, width:] = info.astype(jnp.bfloat16)


def norm(hidden, gain, ids, gates, own, others, padded):
    tok, width = hidden.shape
    return pl.pallas_call(
        norm_kernel,
        out_shape=(
            jax.ShapeDtypeStruct((tok, width), jnp.bfloat16),
            jax.ShapeDtypeStruct((tok, padded), jnp.bfloat16),
        ),
        name="norm",
        compiler_params=pltpu.CompilerParams(vmem_limit_bytes=16 * MIB),
    )(hidden, gain.reshape(1, -1), ids, gates, own, *others)


def small(kernel, name, inputs, shapes, after):
    given = len(inputs)

    def body(*refs):
        kernel(*refs[:given], *refs[given + len(after) : -1])
        refs[-1][...] = jnp.zeros_like(refs[-1])

    moved = sum(x.size for x in inputs) + sum(x.size for x in shapes)
    return pl.pallas_call(
        body,
        out_shape=tuple(shapes) + (TOKEN,),
        in_specs=[pl.BlockSpec(memory_space=VMEM)] * given
        + [pl.BlockSpec(memory_space=pl.ANY)] * len(after),
        out_specs=tuple([pl.BlockSpec(memory_space=VMEM)] * (len(shapes) + 1)),
        compiler_params=pltpu.CompilerParams(vmem_limit_bytes=16 * MIB),
        cost_estimate=LONG,
        name=name,
    )(*inputs, *after)


def rows_like(rows, value):
    return jax.ShapeDtypeStruct((rows, value.shape[1]), value.dtype)


def assemble_kernel(*refs, plan):
    outs = refs[len(refs) - len(plan) :]
    for out, pieces in zip(outs, plan):
        at = 0
        for length, terms in pieces:
            first, start = terms[0]
            total = refs[first][start : start + length]
            if len(terms) > 1:
                total = total.astype(jnp.float32)
                for source, start in terms[1:]:
                    total = total + refs[source][start : start + length].astype(jnp.float32)
            out[at : at + length] = total.astype(out.dtype)
            at += length


def assemble(name, arrays, results, after):
    used = []
    plan = []
    for pieces in results:
        listed = []
        for length, terms in pieces:
            for key, _ in terms:
                if key not in used:
                    used.append(key)
            listed.append((length, tuple((used.index(key), start) for key, start in terms)))
        plan.append(listed)
    inputs = [arrays[key] for key in used]
    shapes = [rows_like(sum(length for length, _ in pieces), inputs[0]) for pieces in plan]
    return small(functools.partial(assemble_kernel, plan=plan), name, inputs, shapes, after)


def experts_kernel(*refs, extra):
    expert, near, far, w_in, w_down = refs[:5]
    out_near, out_far, out_last, token, rows, chosen = refs[5 + extra :]
    half, padded = near.shape
    width = w_down.shape[1]
    count = rows.shape[0] // 2
    segment = 256
    token[...] = jnp.zeros_like(token)
    earlier = (
        lax.broadcasted_iota(jnp.int32, (segment, segment), 0)
        < lax.broadcasted_iota(jnp.int32, (segment, segment), 1)
    ).astype(jnp.float32).astype(jnp.bfloat16)
    weights = []
    for side, source in enumerate((near, far)):
        info = source[:, padded - 128 :].astype(jnp.float32).T
        info = info[128 - (padded - width) :]
        named = info[:TOP] == expert[0]
        picked = jnp.sum(named.astype(jnp.float32), axis=0, keepdims=True)
        gate = info[TOP : 2 * TOP] + info[2 * TOP : 3 * TOP] + info[3 * TOP : 4 * TOP]
        weight = jnp.sum(jnp.where(named, gate, 0.0), axis=0, keepdims=True)
        base = jnp.zeros((1, 1), jnp.float32)
        slots = []
        for at in range(0, half, segment):
            one = picked[:, at : at + segment]
            eight = jnp.broadcast_to(one, (16, segment)).astype(jnp.bfloat16)
            slot = jnp.dot(eight, earlier, preferred_element_type=jnp.float32)[:1]
            slots.append(slot + base)
            base = base + jnp.sum(one, axis=1, keepdims=True)
        slot = jnp.concatenate(slots, axis=1)
        slot = jnp.where(picked > 0.5, slot, -1.0).astype(jnp.int32)
        places = lax.broadcasted_iota(jnp.int32, (count, half), 0) == slot
        chosen[side] = places.astype(jnp.float32).astype(jnp.bfloat16)
        weights.append(jnp.sum(jnp.where(places, weight, 0.0), axis=1, keepdims=True))
        got = jnp.dot(chosen[side], source[:, :width], preferred_element_type=jnp.float32)
        rows[side * count : (side + 1) * count, :] = got.astype(jnp.bfloat16)

    contract_last = (((1,), (1,)), ((), ()))
    gate = lax.dot_general(rows[...], w_in[0], contract_last, preferred_element_type=jnp.float32)
    up = lax.dot_general(rows[...], w_in[1], contract_last, preferred_element_type=jnp.float32)
    hidden = (gate / (1.0 + jnp.exp(-gate)) * up).astype(jnp.bfloat16)
    cut = out_far.shape[0]
    for side in range(2):
        here = hidden[side * count : (side + 1) * count]
        total = jnp.dot(here, w_down[...], preferred_element_type=jnp.float32)
        scaled = (total * weights[side]).astype(jnp.bfloat16)
        spread = lax.dot_general(
            chosen[side], scaled, (((0,), (0,)), ((), ())), preferred_element_type=jnp.float32
        ).astype(jnp.bfloat16)
        if side == 0:
            out_near[:, :width] = spread
        else:
            out_far[:, :width] = spread[:cut]
            out_last[:, :width] = spread[cut:]
    for target in (out_near, out_far, out_last):
        target[:, width:] = jnp.zeros((target.shape[0], padded - width), jnp.bfloat16)


def run_experts(expert, near, far, w_in, w_down, count, after=()):
    half, padded = near.shape
    width = w_down.shape[1]
    vmem = pl.BlockSpec(memory_space=VMEM)
    part = half // 4
    return pl.pallas_call(
        functools.partial(experts_kernel, extra=len(after)),
        out_shape=(
            rows_like(half, near), rows_like(half - part, near), rows_like(part, near), TOKEN
        ),
        in_specs=[pl.BlockSpec(memory_space=SMEM)]
        + [vmem] * 4
        + [pl.BlockSpec(memory_space=pl.ANY)] * len(after),
        out_specs=(vmem, vmem, vmem, vmem),
        scratch_shapes=[
            VMEM((2 * count, width), jnp.bfloat16),
            VMEM((2, count, half), jnp.bfloat16),
        ],
        compiler_params=pltpu.CompilerParams(vmem_limit_bytes=(58 if half > 256 else 36) * MIB),
        cost_estimate=SHORT,
        name="experts",
    )(expert, near, far, w_in, w_down, *after)


def plus(left, right):
    return (left.astype(jnp.float32) + right.astype(jnp.float32)).astype(jnp.bfloat16)


def last_kernel(own, *refs, starts):
    *others, out = refs
    tok, width = out.shape
    step = tok // 4
    for at in range(0, tok, step):
        total = own[at : at + step, :width].astype(jnp.float32)
        for start, other in zip(starts, others):
            if start <= at < start + other.shape[0]:
                here = slice(at - start, at - start + step)
                total = total + other[here, :width].astype(jnp.float32)
        out[at : at + step] = total.astype(jnp.bfloat16)


def per_device(
    hidden_in, qkv_new, kv_cache, cache_len, o_weight, norm_gain,
    expert_ids, gate_weights, w_gate_up, w_down,
):
    seqs = lax.axis_size("seq")
    heads = lax.axis_size("head")
    seq = lax.axis_index("seq")
    head = lax.axis_index("head")
    tok, width = hidden_in.shape
    kv_heads, lanes = qkv_new.shape[1:]
    kv_local = kv_heads // heads
    hd = kv_cache.shape[3] // 2
    gs = lanes // hd - 2
    experts = w_gate_up.shape[0] * seqs
    capacity = max(2, tok * TOP * 5 // (4 * experts))
    padded = -(-(width + 4 * TOP) // 128) * 128

    def along_head(value, mask):
        pairs = [(s * heads + h, s * heads + (h ^ mask)) for s in range(seqs) for h in range(heads)]
        return lax.ppermute(value, AXES, pairs)

    def along_seq(value, mask):
        pairs = [(s * heads + h, (s ^ mask) * heads + h) for s in range(seqs) for h in range(heads)]
        return lax.ppermute(value, AXES, pairs)

    by_group = qkv_new.reshape(tok, heads, kv_local, lanes).transpose(1, 2, 0, 3)
    parts = {
        k: lax.dynamic_index_in_dim(by_group, head ^ k, 0, keepdims=False) for k in range(heads)
    }
    order = list(range(heads - 1, 0, -1))
    for k in order:
        parts[k] = along_head(parts[k], k)
    given = [parts[k] for k in range(heads)]
    cache = jnp.swapaxes(kv_cache[0], 0, 1)
    o_rows = o_weight.T

    def info(k):
        return jnp.stack([cache_len[0], head, head ^ k]).astype(jnp.int32)

    *state, token = attend(
        "start", None, info(0), parts[0], cache, None, o_rows, None, tok, hd, gs
    )
    arrived = []
    for k in order:
        partial, _ = attend(
            "whole", token, info(k), parts[k], cache, given, o_rows, None, tok, hd, gs
        )
        arrived.append(along_head(partial, k))
    own, _ = attend(
        "end", token, info(0), parts[0], cache, given, o_rows, state, tok, hd, gs
    )
    attn_proj, rows = norm(
        hidden_in, norm_gain, expert_ids, gate_weights, own, arrived, padded
    )

    w_in = jnp.transpose(w_gate_up[0], (1, 2, 0))
    expert = seq.astype(jnp.float32).reshape(1)
    plane = {0: rows, 1: along_head(rows, 1), 2: along_head(rows, 2)}
    plane[3] = along_head(plane[2], 1)

    if seqs == 8:
        count = -(-capacity * (seqs // 2) // 16) * 16
        half = tok // 2
        x_at, y_at, low_at, high_at = tok, 2 * tok, 3 * tok, 3 * tok + half
        sequence = [0, 2, 3, 1]
        got = {f"p{i}": plane[k] for i, k in enumerate(sequence)}
        far = {}
        w_local = w_down[0]
        latest = [jnp.zeros(TOKEN.shape, TOKEN.dtype)]

        def exchange(stage, to_x, to_y):
            got[f"x{stage}"] = along_seq(to_x, 2)
            got[f"y{stage}"] = along_seq(to_y, 4)

        def run(name, results):
            *made, latest[0] = assemble(name, got, results, latest)
            del latest[1:]
            return made

        def send(name, stage, to_x, to_y, *results):
            made = run(name, [to_x, to_y, *results])
            exchange(stage, made[0], made[1])
            return made[2:]

        def experts_of(k):
            got[f"b{k}"], rest, corner, latest[0] = run_experts(
                expert, got[f"n{k}"], far[k], w_in, w_local, count, latest
            )
            got[f"r{k}"] = along_seq(rest, 1)
            got[f"c{k}"] = along_seq(corner, 1)

        def summed(k, start, length, *more):
            other = (f"r{k}", start) if start < low_at else (f"c{k}", start - low_at)
            return (length, [(f"b{k}", start), other, *more])

        def corner_of(stage, at):
            return [(half, [(f"y{stage}", at)]), (half, [(f"x{stage}", at)])]

        def pack(k, corner):
            pieces = [(tok, [(f"{name}{k}", 0)]) for name in "pxy"] + corner
            (got[f"n{k}"],) = run("pack", [pieces])
            far[k] = along_seq(got[f"n{k}"], 1)

        def returned(k, stage, at):
            return (
                [summed(k, x_at, half, (f"y{stage}", at)), summed(k, x_at + half, half)],
                [summed(k, y_at, half), summed(k, y_at + half, half, (f"x{stage}", at))],
            )

        def finished(k, stage, at=0, length=tok):
            return [summed(k, at, length, (f"x{stage}", at), (f"y{stage}", at))]

        exchange(0, rows, rows)
        send(
            "gather", 1,
            [(tok, [("p1", 0)]), (half, [("y0", half)])],
            [(tok, [("p1", 0)]), (half, [("x0", 0)])],
        )
        neighbour_x = along_head(got["x0"], 1)
        (corner,) = send(
            "gather", 2,
            [(tok, [("p2", 0)]), (half, [("y1", half)])],
            [(tok, [("p2", 0)]), (half, [("x1", 0)])],
            corner_of(1, tok),
        )
        neighbour_y = along_head(got["y0"], 1)
        pack(0, corner_of(1, tok))
        experts_of(0)
        latest += [neighbour_x, neighbour_y]
        send(
            "turn", 3,
            [(half, [("y2", half)]), summed(0, high_at, half)],
            [(half, [("x2", 0)]), summed(0, low_at, half)],
        )
        neighbour_corner = along_head(corner, 1)
        pack(1, corner_of(2, tok))
        experts_of(1)
        latest.append(neighbour_corner)
        to_x, to_y = returned(0, 3, half)
        send(
            "turn", 4, to_x + [summed(1, high_at, half)], to_y + [summed(1, low_at, half)]
        )
        pack(2, corner_of(3, 0))
        got["nx"], got["ny"], got["nc"] = neighbour_x, neighbour_y, neighbour_corner
        (got["n3"],) = run("pack", [[(tok, [(key, 0)]) for key in ("p3", "nx", "ny", "nc")]])
        far[3] = along_seq(got["n3"], 1)
        experts_of(2)
        to_x, to_y = returned(1, 4, tok)
        (own_rows,) = send(
            "reduce", 5,
            to_x + [summed(2, high_at, half)],
            to_y + [summed(2, low_at, half)],
            finished(0, 4),
        )
        experts_of(3)
        to_x, to_y = returned(2, 5, tok)
        cut = 3 * tok // 4
        made = send(
            "reduce", 6,
            to_x + [summed(3, high_at, half)],
            to_y + [summed(3, low_at, half)],
            finished(1, 5, 0, cut),
            finished(1, 5, cut, tok - cut),
        )
        others = [(0, along_head(made[0], sequence[1])), (cut, along_head(made[1], sequence[1]))]
        latest.append(others[0][1])
        to_x, to_y = returned(3, 6, tok)
        (made,) = send("reduce", 7, to_x, to_y, finished(2, 6))
        others.append((0, along_head(made, sequence[2])))
        (made,) = run("reduce", [finished(3, 7)])
        others.append((0, along_head(made, sequence[3])))
    else:
        masks = [1 << b for b in range(1, seqs.bit_length() - 1)]
        count = -(-capacity * (seqs // 2) // 16) * 16
        done = []
        for k in range(4):
            near = plane[k]
            for mask in masks:
                near = jnp.concatenate([near, along_seq(near, mask)], axis=0)
            far = along_seq(near, 1)
            near, far, rest, _ = run_experts(expert, near, far, w_in, w_down[0], count)
            far = jnp.concatenate([far, rest], axis=0)
            near = plus(near, along_seq(far, 1))
            for mask in masks[::-1]:
                cut = near.shape[0] // 2
                near = plus(near[:cut], along_seq(near[cut:], mask))
            done.append(near)
        own_rows = done[0]
        others = [(0, along_head(done[k], k)) for k in range(1, heads)]
    moe = pl.pallas_call(
        functools.partial(last_kernel, starts=[at for at, _ in others]),
        out_shape=jax.ShapeDtypeStruct((tok, width), jnp.bfloat16),
        name="last",
    )(own_rows, *[value for _, value in others])
    return attn_proj, moe


def solution(mesh):
    return jax.shard_map(
        per_device,
        mesh=mesh,
        in_specs=(
            P(("seq", "head"), None),
            P(("seq", "head"), None, None),
            P("seq", None, "head", None),
            P("seq"),
            P("head", None),
            P(),
            P(("seq", "head"), None),
            P(("seq", "head"), None),
            P("seq", None, None, "head"),
            P("seq", "head", None),
        ),
        out_specs=(P(("seq", "head"), None), P(("seq", "head"), None)),
        check_vma=False,
    )
```

```python
import functools

import jax
import jax.numpy as jnp
from jax import lax
from jax.experimental import pallas as pl
from jax.experimental.pallas import tpu as pltpu
from jax.sharding import PartitionSpec as P

TOP = 4
EPSILON = 1e-05
LOG2E = 1.4426950408889634
FLOOR = -1e30
AXES = ("seq", "head")
MIB = 2**20
TOKEN = jax.ShapeDtypeStruct((8, 128), jnp.float32)
VMEM = pltpu.VMEM
LONG = pl.CostEstimate(flops=2 * 10**10, bytes_accessed=10**8, transcendentals=0)
SHORT = pl.CostEstimate(flops=1, bytes_accessed=1, transcendentals=0)
SMEM = pltpu.SMEM


def key_block(cached):
    return 2048 if cached % 2048 == 0 else cached


def attend_kernel(*refs, tok, hd, gs, bk, cached, mode):
    refs = list(refs)
    if mode != "start":
        refs.pop(0)
    info = refs.pop(0)
    chunk = refs.pop(0)
    cache_far = refs.pop(0)
    if mode != "start":
        parts = [refs.pop(0) for _ in range(4)]
        o_weight = refs.pop(0)
    if mode == "end":
        acc_in, top_in = refs.pop(0), refs.pop(0)
    if mode == "start":
        acc, top, token = refs.pop(0), refs.pop(0), refs.pop(0)
        queries, cache, sems = refs
    else:
        out, token = refs.pop(0), refs.pop(0)
        acc, top, queries, cache, o_local, sems = refs
    token[...] = jnp.zeros_like(token)
    heads = cache.shape[0]
    blocks = cached // bk
    live, mine, asked = info[0], info[1], info[2]
    last = (live - 1) // bk

    def cache_copy(index):
        here = pl.ds(pl.multiple_of(index * bk, bk), bk)
        return pltpu.make_async_copy(cache_far.at[:, here], cache.at[:, here], sems.at[index])

    def begin(index, carry):
        cache_copy(index).start()
        return carry

    first_block = last if mode == "end" else 0
    lax.fori_loop(first_block, last if mode == "start" else last + 1, begin, 0)
    if mode != "start":
        o_copy = pltpu.make_async_copy(o_weight, o_local, sems.at[blocks])
        o_copy.start()
    for h in range(heads):
        for r in range(gs):
            one = chunk[h, :, r * hd : (r + 1) * hd] * jnp.bfloat16(hd**-0.5)
            queries[h, r * tok : (r + 1) * tok, :] = jnp.concatenate(
                [one, jnp.zeros_like(one)], axis=1
            )
    lane = lax.broadcasted_iota(jnp.int32, (1, 2 * hd), 1)
    is_value = (lane >= hd).astype(jnp.float32).astype(jnp.bfloat16)
    is_key = (lane < hd).astype(jnp.float32).astype(jnp.bfloat16)
    if mode == "end":
        acc[...] = acc_in[...]
        top[...] = top_in[...]
    elif mode == "start":
        acc[...] = jnp.zeros_like(acc)
        top[...] = jnp.full_like(top, FLOOR)

    def block(h, keys, mask):
        scores = lax.dot_general(
            queries[h], keys, (((1,), (1,)), ((), ())), preferred_element_type=jnp.float32
        )
        if mask is not None:
            scores = jnp.where(mask(scores.shape), scores, FLOOR)
        return scores

    def absorb(h, keys, scores, empty=False):
        values = keys * is_value + is_key
        largest = jnp.max(scores, axis=1, keepdims=True)
        if empty:
            now = jnp.broadcast_to(largest, top.shape[1:])
        else:
            before = top[h]
            now = jnp.maximum(before, largest)
        weights = jnp.exp2((scores - now[:, :1]) * LOG2E).astype(jnp.bfloat16)
        part = jnp.dot(weights, values, preferred_element_type=jnp.float32)
        acc[h] = part if empty else acc[h] * jnp.exp2((before - now) * LOG2E) + part
        top[h] = now

    def causal(shape):
        column = lax.broadcasted_iota(jnp.int32, shape, 1)
        row = lax.broadcasted_iota(jnp.int32, shape, 0)
        where = (mine ^ (column // tok)) * tok + column % tok
        return where <= asked * tok + row % tok

    def new_keys():
        fresh = [
            jnp.concatenate([part[h, :, gs * hd :] for part in parts], axis=0)
            for h in range(heads)
        ]
        scores = [block(h, fresh[h], causal) for h in range(heads)]
        for h in range(heads):
            absorb(h, fresh[h], scores[h], mode == "whole")

    def cached_step(index, masked):
        start = pl.multiple_of(index * bk, bk)
        cache_copy(index).wait()
        keys = [cache[h, pl.ds(start, bk), :] for h in range(heads)]

        def alive(shape):
            return lax.broadcasted_iota(jnp.int32, shape, 1) + start < live

        scores = [block(h, keys[h], alive if masked else None) for h in range(heads)]
        for h in range(heads):
            absorb(h, keys[h], scores[h])

    def body(index, carry):
        cached_step(index, False)
        return carry

    if mode != "start":
        new_keys()
    full = last if mode == "start" else live // bk
    lax.fori_loop(first_block, full, body, 0)
    if mode == "start":
        return

    @pl.when(full * bk < live)
    def _():
        cached_step(full, True)

    pieces = []
    for h in range(heads):
        total = acc[h]
        done = (total[:, hd:] / total[:, :hd]).astype(jnp.bfloat16)
        pieces += [done[r * tok : (r + 1) * tok] for r in range(gs)]
    attention = jnp.concatenate(pieces, axis=1)
    o_copy.wait()
    turned = lax.dot_general(
        o_local[...], attention, (((1,), (1,)), ((), ())), preferred_element_type=jnp.float32
    )
    out[...] = turned.T.astype(out.dtype)


def attend(mode, after, info, chunk, cache, parts, o_rows, state, tok, hd, gs):
    heads, cached, lanes = cache.shape
    width, depth = o_rows.shape
    bk = key_block(cached)
    vmem = pl.BlockSpec(memory_space=VMEM)
    anywhere = pl.BlockSpec(memory_space=pl.ANY)
    inputs, specs = [info, chunk, cache], [pl.BlockSpec(memory_space=SMEM), vmem, anywhere]
    if mode != "start":
        inputs += [*parts, o_rows]
        specs += [vmem] * 4 + [anywhere]
    if mode == "end":
        inputs += list(state)
        specs += [vmem] * 2
    if mode != "start":
        inputs, specs = [after] + inputs, [anywhere] + specs
    held = (heads, tok * gs, lanes)
    state_shape = jax.ShapeDtypeStruct(held, jnp.float32)
    scratch = [
        VMEM(held, jnp.bfloat16),
        VMEM(cache.shape, jnp.bfloat16),
        pltpu.SemaphoreType.DMA((cached // bk + 1,)),
    ]
    if mode != "start":
        scratch = [VMEM(held, jnp.float32)] * 2 + scratch
        scratch.insert(4, VMEM((width, depth), jnp.bfloat16))
    return pl.pallas_call(
        functools.partial(
            attend_kernel, tok=tok, hd=hd, gs=gs, bk=bk, cached=cached, mode=mode
        ),
        out_shape=(state_shape, state_shape, TOKEN)
        if mode == "start"
        else (jax.ShapeDtypeStruct((tok, width), jnp.bfloat16), TOKEN),
        in_specs=specs,
        out_specs=(vmem,) * (3 if mode == "start" else 2),
        scratch_shapes=scratch,
        compiler_params=pltpu.CompilerParams(vmem_limit_bytes=48 * MIB),
        cost_estimate=SHORT,
        name="attend_" + mode,
    )(*inputs)


def norm_kernel(hidden, gain, ids, gates, own, *refs):
    *others, proj, out = refs
    width = hidden.shape[1]
    total = own[...].astype(jnp.float32)
    for other in others:
        total = total + other[...].astype(jnp.float32)
    rounded = total.astype(jnp.bfloat16)
    proj[...] = rounded
    residual = (hidden[...].astype(jnp.float32) + rounded.astype(jnp.float32)).astype(jnp.bfloat16)
    wide = residual.astype(jnp.float32)
    mean = jnp.mean(wide * wide, axis=1, keepdims=True)
    out[:, :width] = (wide * lax.rsqrt(mean + EPSILON) * gain[...]).astype(jnp.bfloat16)
    gate = gates[...]
    high = gate.astype(jnp.bfloat16).astype(jnp.float32)
    middle = (gate - high).astype(jnp.bfloat16).astype(jnp.float32)
    low = gate - high - middle
    spare = jnp.zeros((hidden.shape[0], out.shape[1] - width - 4 * TOP), jnp.float32)
    info = jnp.concatenate([ids[...].astype(jnp.float32), high, middle, low, spare], axis=1)
    out[:, width:] = info.astype(jnp.bfloat16)


def norm(hidden, gain, ids, gates, own, others, padded):
    tok, width = hidden.shape
    return pl.pallas_call(
        norm_kernel,
        out_shape=(
            jax.ShapeDtypeStruct((tok, width), jnp.bfloat16),
            jax.ShapeDtypeStruct((tok, padded), jnp.bfloat16),
        ),
        name="norm",
        compiler_params=pltpu.CompilerParams(vmem_limit_bytes=16 * MIB),
    )(hidden, gain.reshape(1, -1), ids, gates, own, *others)


def small(kernel, name, inputs, shapes, after):
    given = len(inputs)

    def body(*refs):
        kernel(*refs[:given], *refs[given + len(after) : -1])
        refs[-1][...] = jnp.zeros_like(refs[-1])

    moved = sum(x.size for x in inputs) + sum(x.size for x in shapes)
    return pl.pallas_call(
        body,
        out_shape=tuple(shapes) + (TOKEN,),
        in_specs=[pl.BlockSpec(memory_space=VMEM)] * given
        + [pl.BlockSpec(memory_space=pl.ANY)] * len(after),
        out_specs=tuple([pl.BlockSpec(memory_space=VMEM)] * (len(shapes) + 1)),
        compiler_params=pltpu.CompilerParams(vmem_limit_bytes=16 * MIB),
        cost_estimate=LONG,
        name=name,
    )(*inputs, *after)


def rows_like(rows, value):
    return jax.ShapeDtypeStruct((rows, value.shape[1]), value.dtype)


def assemble_kernel(*refs, plan):
    outs = refs[len(refs) - len(plan) :]
    for out, pieces in zip(outs, plan):
        at = 0
        for length, terms in pieces:
            first, start = terms[0]
            total = refs[first][start : start + length]
            if len(terms) > 1:
                total = total.astype(jnp.float32)
                for source, start in terms[1:]:
                    total = total + refs[source][start : start + length].astype(jnp.float32)
            out[at : at + length] = total.astype(out.dtype)
            at += length


def assemble(name, arrays, results, after):
    used = []
    plan = []
    for pieces in results:
        listed = []
        for length, terms in pieces:
            for key, _ in terms:
                if key not in used:
                    used.append(key)
            listed.append((length, tuple((used.index(key), start) for key, start in terms)))
        plan.append(listed)
    inputs = [arrays[key] for key in used]
    shapes = [rows_like(sum(length for length, _ in pieces), inputs[0]) for pieces in plan]
    return small(functools.partial(assemble_kernel, plan=plan), name, inputs, shapes, after)


def experts_kernel(*refs, extra):
    expert, near, far, w_in, w_down = refs[:5]
    out_near, out_far, out_last, token, rows, chosen = refs[5 + extra :]
    half, padded = near.shape
    width = w_down.shape[1]
    count = rows.shape[0] // 2
    segment = 256
    token[...] = jnp.zeros_like(token)
    earlier = (
        lax.broadcasted_iota(jnp.int32, (segment, segment), 0)
        < lax.broadcasted_iota(jnp.int32, (segment, segment), 1)
    ).astype(jnp.float32).astype(jnp.bfloat16)
    weights = []
    for side, source in enumerate((near, far)):
        info = source[:, padded - 128 :].astype(jnp.float32).T
        info = info[128 - (padded - width) :]
        named = info[:TOP] == expert[0]
        picked = jnp.sum(named.astype(jnp.float32), axis=0, keepdims=True)
        gate = info[TOP : 2 * TOP] + info[2 * TOP : 3 * TOP] + info[3 * TOP : 4 * TOP]
        weight = jnp.sum(jnp.where(named, gate, 0.0), axis=0, keepdims=True)
        base = jnp.zeros((1, 1), jnp.float32)
        slots = []
        for at in range(0, half, segment):
            one = picked[:, at : at + segment]
            eight = jnp.broadcast_to(one, (16, segment)).astype(jnp.bfloat16)
            slot = jnp.dot(eight, earlier, preferred_element_type=jnp.float32)[:1]
            slots.append(slot + base)
            base = base + jnp.sum(one, axis=1, keepdims=True)
        slot = jnp.concatenate(slots, axis=1)
        slot = jnp.where(picked > 0.5, slot, -1.0).astype(jnp.int32)
        places = lax.broadcasted_iota(jnp.int32, (count, half), 0) == slot
        chosen[side] = places.astype(jnp.float32).astype(jnp.bfloat16)
        weights.append(jnp.sum(jnp.where(places, weight, 0.0), axis=1, keepdims=True))
        got = jnp.dot(chosen[side], source[:, :width], preferred_element_type=jnp.float32)
        rows[side * count : (side + 1) * count, :] = got.astype(jnp.bfloat16)

    contract_last = (((1,), (1,)), ((), ()))
    gate = lax.dot_general(rows[...], w_in[0], contract_last, preferred_element_type=jnp.float32)
    up = lax.dot_general(rows[...], w_in[1], contract_last, preferred_element_type=jnp.float32)
    hidden = (gate / (1.0 + jnp.exp(-gate)) * up).astype(jnp.bfloat16)
    cut = out_far.shape[0]
    for side in range(2):
        here = hidden[side * count : (side + 1) * count]
        total = jnp.dot(here, w_down[...], preferred_element_type=jnp.float32)
        scaled = (total * weights[side]).astype(jnp.bfloat16)
        spread = lax.dot_general(
            chosen[side], scaled, (((0,), (0,)), ((), ())), preferred_element_type=jnp.float32
        ).astype(jnp.bfloat16)
        if side == 0:
            out_near[:, :width] = spread
        else:
            out_far[:, :width] = spread[:cut]
            out_last[:, :width] = spread[cut:]
    for target in (out_near, out_far, out_last):
        target[:, width:] = jnp.zeros((target.shape[0], padded - width), jnp.bfloat16)


def run_experts(expert, near, far, w_in, w_down, count, after=()):
    half, padded = near.shape
    width = w_down.shape[1]
    vmem = pl.BlockSpec(memory_space=VMEM)
    part = half // 4
    return pl.pallas_call(
        functools.partial(experts_kernel, extra=len(after)),
        out_shape=(
            rows_like(half, near), rows_like(half - part, near), rows_like(part, near), TOKEN
        ),
        in_specs=[pl.BlockSpec(memory_space=SMEM)]
        + [vmem] * 4
        + [pl.BlockSpec(memory_space=pl.ANY)] * len(after),
        out_specs=(vmem, vmem, vmem, vmem),
        scratch_shapes=[
            VMEM((2 * count, width), jnp.bfloat16),
            VMEM((2, count, half), jnp.bfloat16),
        ],
        compiler_params=pltpu.CompilerParams(vmem_limit_bytes=(58 if half > 256 else 36) * MIB),
        cost_estimate=SHORT,
        name="experts",
    )(expert, near, far, w_in, w_down, *after)


def plus(left, right):
    return (left.astype(jnp.float32) + right.astype(jnp.float32)).astype(jnp.bfloat16)


def last_kernel(own, *refs, starts):
    *others, out = refs
    tok, width = out.shape
    step = tok // 4
    for at in range(0, tok, step):
        total = own[at : at + step, :width].astype(jnp.float32)
        for start, other in zip(starts, others):
            if start <= at < start + other.shape[0]:
                here = slice(at - start, at - start + step)
                total = total + other[here, :width].astype(jnp.float32)
        out[at : at + step] = total.astype(jnp.bfloat16)


def per_device(
    hidden_in, qkv_new, kv_cache, cache_len, o_weight, norm_gain,
    expert_ids, gate_weights, w_gate_up, w_down,
):
    seqs = lax.axis_size("seq")
    heads = lax.axis_size("head")
    seq = lax.axis_index("seq")
    head = lax.axis_index("head")
    tok, width = hidden_in.shape
    kv_heads, lanes = qkv_new.shape[1:]
    kv_local = kv_heads // heads
    hd = kv_cache.shape[3] // 2
    gs = lanes // hd - 2
    experts = w_gate_up.shape[0] * seqs
    capacity = max(2, tok * TOP * 5 // (4 * experts))
    padded = -(-(width + 4 * TOP) // 128) * 128

    def along_head(value, mask):
        pairs = [(s * heads + h, s * heads + (h ^ mask)) for s in range(seqs) for h in range(heads)]
        return lax.ppermute(value, AXES, pairs)

    def along_seq(value, mask):
        pairs = [(s * heads + h, (s ^ mask) * heads + h) for s in range(seqs) for h in range(heads)]
        return lax.ppermute(value, AXES, pairs)

    by_group = qkv_new.reshape(tok, heads, kv_local, lanes).transpose(1, 2, 0, 3)
    parts = {
        k: lax.dynamic_index_in_dim(by_group, head ^ k, 0, keepdims=False) for k in range(heads)
    }
    order = list(range(heads - 1, 0, -1))
    for k in order:
        parts[k] = along_head(parts[k], k)
    given = [parts[k] for k in range(heads)]
    cache = jnp.swapaxes(kv_cache[0], 0, 1)
    o_rows = o_weight.T

    def info(k):
        return jnp.stack([cache_len[0], head, head ^ k]).astype(jnp.int32)

    *state, token = attend(
        "start", None, info(0), parts[0], cache, None, o_rows, None, tok, hd, gs
    )
    arrived = []
    for k in order:
        partial, _ = attend(
            "whole", token, info(k), parts[k], cache, given, o_rows, None, tok, hd, gs
        )
        arrived.append(along_head(partial, k))
    own, _ = attend(
        "end", token, info(0), parts[0], cache, given, o_rows, state, tok, hd, gs
    )
    attn_proj, rows = norm(
        hidden_in, norm_gain, expert_ids, gate_weights, own, arrived, padded
    )

    w_in = jnp.transpose(w_gate_up[0], (1, 2, 0))
    expert = seq.astype(jnp.float32).reshape(1)
    plane = {0: rows, 1: along_head(rows, 1), 2: along_head(rows, 2)}
    plane[3] = along_head(plane[2], 1)

    if seqs == 8:
        count = -(-capacity * (seqs // 2) // 16) * 16
        half = tok // 2
        x_at, y_at, low_at, high_at = tok, 2 * tok, 3 * tok, 3 * tok + half
        sequence = [0, 2, 3, 1]
        got = {f"p{i}": plane[k] for i, k in enumerate(sequence)}
        far = {}
        w_local = w_down[0]
        latest = [jnp.zeros(TOKEN.shape, TOKEN.dtype)]

        def exchange(stage, to_x, to_y):
            got[f"x{stage}"] = along_seq(to_x, 2)
            got[f"y{stage}"] = along_seq(to_y, 4)

        def run(name, results):
            *made, latest[0] = assemble(name, got, results, latest)
            del latest[1:]
            return made

        def send(name, stage, to_x, to_y, *results):
            made = run(name, [to_x, to_y, *results])
            exchange(stage, made[0], made[1])
            return made[2:]

        def experts_of(k):
            got[f"b{k}"], rest, corner, latest[0] = run_experts(
                expert, got[f"n{k}"], far[k], w_in, w_local, count, latest
            )
            got[f"r{k}"] = along_seq(rest, 1)
            got[f"c{k}"] = along_seq(corner, 1)

        def summed(k, start, length, *more):
            other = (f"r{k}", start) if start < low_at else (f"c{k}", start - low_at)
            return (length, [(f"b{k}", start), other, *more])

        def corner_of(stage, at):
            return [(half, [(f"y{stage}", at)]), (half, [(f"x{stage}", at)])]

        def pack(k, corner):
            pieces = [(tok, [(f"{name}{k}", 0)]) for name in "pxy"] + corner
            (got[f"n{k}"],) = run("pack", [pieces])
            far[k] = along_seq(got[f"n{k}"], 1)

        def returned(k, stage, at):
            return (
                [summed(k, x_at, half, (f"y{stage}", at)), summed(k, x_at + half, half)],
                [summed(k, y_at, half), summed(k, y_at + half, half, (f"x{stage}", at))],
            )

        def finished(k, stage, at=0, length=tok):
            return [summed(k, at, length, (f"x{stage}", at), (f"y{stage}", at))]

        exchange(0, rows, rows)
        latest.append(got["p3"])
        send(
            "gather", 1,
            [(tok, [("p1", 0)]), (half, [("y0", half)])],
            [(tok, [("p1", 0)]), (half, [("x0", 0)])],
        )
        neighbour_x = along_head(got["x0"], 1)
        (corner,) = send(
            "gather", 2,
            [(tok, [("p2", 0)]), (half, [("y1", half)])],
            [(tok, [("p2", 0)]), (half, [("x1", 0)])],
            corner_of(1, tok),
        )
        neighbour_y = along_head(got["y0"], 1)
        pack(0, corner_of(1, tok))
        experts_of(0)
        latest += [neighbour_x, neighbour_y]
        send(
            "turn", 3,
            [(half, [("y2", half)]), summed(0, high_at, half)],
            [(half, [("x2", 0)]), summed(0, low_at, half)],
        )
        neighbour_corner = along_head(corner, 1)
        pack(1, corner_of(2, tok))
        experts_of(1)
        latest.append(neighbour_corner)
        to_x, to_y = returned(0, 3, half)
        send(
            "turn", 4, to_x + [summed(1, high_at, half)], to_y + [summed(1, low_at, half)]
        )
        pack(2, corner_of(3, 0))
        got["nx"], got["ny"], got["nc"] = neighbour_x, neighbour_y, neighbour_corner
        (got["n3"],) = run("pack", [[(tok, [(key, 0)]) for key in ("p3", "nx", "ny", "nc")]])
        far[3] = along_seq(got["n3"], 1)
        experts_of(2)
        to_x, to_y = returned(1, 4, tok)
        (own_rows,) = send(
            "reduce", 5,
            to_x + [summed(2, high_at, half)],
            to_y + [summed(2, low_at, half)],
            finished(0, 4),
        )
        experts_of(3)
        to_x, to_y = returned(2, 5, tok)
        cut = 3 * tok // 4
        made = send(
            "reduce", 6,
            to_x + [summed(3, high_at, half)],
            to_y + [summed(3, low_at, half)],
            finished(1, 5, 0, cut),
            finished(1, 5, cut, tok - cut),
        )
        others = [(0, along_head(made[0], sequence[1])), (cut, along_head(made[1], sequence[1]))]
        latest.append(others[0][1])
        to_x, to_y = returned(3, 6, tok)
        (made,) = send("reduce", 7, to_x, to_y, finished(2, 6))
        others.append((0, along_head(made, sequence[2])))
        (made,) = run("reduce", [finished(3, 7)])
        others.append((0, along_head(made, sequence[3])))
    else:
        masks = [1 << b for b in range(1, seqs.bit_length() - 1)]
        count = -(-capacity * (seqs // 2) // 16) * 16
        done = []
        for k in range(4):
            near = plane[k]
            for mask in masks:
                near = jnp.concatenate([near, along_seq(near, mask)], axis=0)
            far = along_seq(near, 1)
            near, far, rest, _ = run_experts(expert, near, far, w_in, w_down[0], count)
            far = jnp.concatenate([far, rest], axis=0)
            near = plus(near, along_seq(far, 1))
            for mask in masks[::-1]:
                cut = near.shape[0] // 2
                near = plus(near[:cut], along_seq(near[cut:], mask))
            done.append(near)
        own_rows = done[0]
        others = [(0, along_head(done[k], k)) for k in range(1, heads)]
    moe = pl.pallas_call(
        functools.partial(last_kernel, starts=[at for at, _ in others]),
        out_shape=jax.ShapeDtypeStruct((tok, width), jnp.bfloat16),
        name="last",
    )(own_rows, *[value for _, value in others])
    return attn_proj, moe


def solution(mesh):
    return jax.shard_map(
        per_device,
        mesh=mesh,
        in_specs=(
            P(("seq", "head"), None),
            P(("seq", "head"), None, None),
            P("seq", None, "head", None),
            P("seq"),
            P("head", None),
            P(),
            P(("seq", "head"), None),
            P(("seq", "head"), None),
            P("seq", None, None, "head"),
            P("seq", "head", None),
        ),
        out_specs=(P(("seq", "head"), None), P(("seq", "head"), None)),
        check_vma=False,
    )
```

```python
import functools

import jax
import jax.numpy as jnp
from jax import lax
from jax.experimental import pallas as pl
from jax.experimental.pallas import tpu as pltpu
from jax.sharding import PartitionSpec as P

TOP = 4
EPSILON = 1e-05
LOG2E = 1.4426950408889634
FLOOR = -1e30
AXES = ("seq", "head")
MIB = 2**20
TOKEN = jax.ShapeDtypeStruct((8, 128), jnp.float32)
VMEM = pltpu.VMEM
LONG = pl.CostEstimate(flops=2 * 10**10, bytes_accessed=10**8, transcendentals=0)
SHORT = pl.CostEstimate(flops=1, bytes_accessed=1, transcendentals=0)
SMEM = pltpu.SMEM


def key_block(cached):
    return 2048 if cached % 2048 == 0 else cached


def attend_kernel(*refs, tok, hd, gs, bk, cached, mode):
    refs = list(refs)
    if mode != "start":
        refs.pop(0)
    info = refs.pop(0)
    chunk = refs.pop(0)
    cache_far = refs.pop(0)
    if mode != "start":
        parts = [refs.pop(0) for _ in range(4)]
        o_weight = refs.pop(0)
    if mode == "end":
        acc_in, top_in = refs.pop(0), refs.pop(0)
    if mode == "start":
        acc, top, token = refs.pop(0), refs.pop(0), refs.pop(0)
        queries, cache, sems = refs
    else:
        out, token = refs.pop(0), refs.pop(0)
        acc, top, queries, cache, o_local, sems = refs
    token[...] = jnp.zeros_like(token)
    heads = cache.shape[0]
    blocks = cached // bk
    live, mine, asked = info[0], info[1], info[2]
    last = (live - 1) // bk

    def cache_copy(index):
        here = pl.ds(pl.multiple_of(index * bk, bk), bk)
        return pltpu.make_async_copy(cache_far.at[:, here], cache.at[:, here], sems.at[index])

    def begin(index, carry):
        cache_copy(index).start()
        return carry

    first_block = last if mode == "end" else 0
    lax.fori_loop(first_block, last if mode == "start" else last + 1, begin, 0)
    if mode != "start":
        o_copy = pltpu.make_async_copy(o_weight, o_local, sems.at[blocks])
        o_copy.start()
    for h in range(heads):
        for r in range(gs):
            one = chunk[h, :, r * hd : (r + 1) * hd] * jnp.bfloat16(hd**-0.5)
            queries[h, r * tok : (r + 1) * tok, :] = jnp.concatenate(
                [one, jnp.zeros_like(one)], axis=1
            )
    lane = lax.broadcasted_iota(jnp.int32, (1, 2 * hd), 1)
    is_value = (lane >= hd).astype(jnp.float32).astype(jnp.bfloat16)
    is_key = (lane < hd).astype(jnp.float32).astype(jnp.bfloat16)
    if mode == "end":
        acc[...] = acc_in[...]
        top[...] = top_in[...]
    elif mode == "start":
        acc[...] = jnp.zeros_like(acc)
        top[...] = jnp.full_like(top, FLOOR)

    def block(h, keys, mask):
        scores = lax.dot_general(
            queries[h], keys, (((1,), (1,)), ((), ())), preferred_element_type=jnp.float32
        )
        if mask is not None:
            scores = jnp.where(mask(scores.shape), scores, FLOOR)
        return scores

    def absorb(h, keys, scores, empty=False):
        values = keys * is_value + is_key
        largest = jnp.max(scores, axis=1, keepdims=True)
        if empty:
            now = jnp.broadcast_to(largest, top.shape[1:])
        else:
            before = top[h]
            now = jnp.maximum(before, largest)
        weights = jnp.exp2((scores - now[:, :1]) * LOG2E).astype(jnp.bfloat16)
        part = jnp.dot(weights, values, preferred_element_type=jnp.float32)
        acc[h] = part if empty else acc[h] * jnp.exp2((before - now) * LOG2E) + part
        top[h] = now

    def causal(shape):
        column = lax.broadcasted_iota(jnp.int32, shape, 1)
        row = lax.broadcasted_iota(jnp.int32, shape, 0)
        where = (mine ^ (column // tok)) * tok + column % tok
        return where <= asked * tok + row % tok

    def new_keys():
        fresh = [
            jnp.concatenate([part[h, :, gs * hd :] for part in parts], axis=0)
            for h in range(heads)
        ]
        scores = [block(h, fresh[h], causal) for h in range(heads)]
        for h in range(heads):
            absorb(h, fresh[h], scores[h], mode == "whole")

    def cached_step(index, masked):
        start = pl.multiple_of(index * bk, bk)
        cache_copy(index).wait()
        keys = [cache[h, pl.ds(start, bk), :] for h in range(heads)]

        def alive(shape):
            return lax.broadcasted_iota(jnp.int32, shape, 1) + start < live

        scores = [block(h, keys[h], alive if masked else None) for h in range(heads)]
        for h in range(heads):
            absorb(h, keys[h], scores[h])

    def body(index, carry):
        cached_step(index, False)
        return carry

    if mode != "start":
        new_keys()
    full = last if mode == "start" else live // bk
    lax.fori_loop(first_block, full, body, 0)
    if mode == "start":
        return

    @pl.when(full * bk < live)
    def _():
        cached_step(full, True)

    pieces = []
    for h in range(heads):
        total = acc[h]
        done = (total[:, hd:] / total[:, :hd]).astype(jnp.bfloat16)
        pieces += [done[r * tok : (r + 1) * tok] for r in range(gs)]
    attention = jnp.concatenate(pieces, axis=1)
    o_copy.wait()
    turned = lax.dot_general(
        o_local[...], attention, (((1,), (1,)), ((), ())), preferred_element_type=jnp.float32
    )
    out[...] = turned.T.astype(out.dtype)


def attend(mode, after, info, chunk, cache, parts, o_rows, state, tok, hd, gs):
    heads, cached, lanes = cache.shape
    width, depth = o_rows.shape
    bk = key_block(cached)
    vmem = pl.BlockSpec(memory_space=VMEM)
    anywhere = pl.BlockSpec(memory_space=pl.ANY)
    inputs, specs = [info, chunk, cache], [pl.BlockSpec(memory_space=SMEM), vmem, anywhere]
    if mode != "start":
        inputs += [*parts, o_rows]
        specs += [vmem] * 4 + [anywhere]
    if mode == "end":
        inputs += list(state)
        specs += [vmem] * 2
    if mode != "start":
        inputs, specs = [after] + inputs, [anywhere] + specs
    held = (heads, tok * gs, lanes)
    state_shape = jax.ShapeDtypeStruct(held, jnp.float32)
    scratch = [
        VMEM(held, jnp.bfloat16),
        VMEM(cache.shape, jnp.bfloat16),
        pltpu.SemaphoreType.DMA((cached // bk + 1,)),
    ]
    if mode != "start":
        scratch = [VMEM(held, jnp.float32)] * 2 + scratch
        scratch.insert(4, VMEM((width, depth), jnp.bfloat16))
    return pl.pallas_call(
        functools.partial(
            attend_kernel, tok=tok, hd=hd, gs=gs, bk=bk, cached=cached, mode=mode
        ),
        out_shape=(state_shape, state_shape, TOKEN)
        if mode == "start"
        else (jax.ShapeDtypeStruct((tok, width), jnp.bfloat16), TOKEN),
        in_specs=specs,
        out_specs=(vmem,) * (3 if mode == "start" else 2),
        scratch_shapes=scratch,
        compiler_params=pltpu.CompilerParams(vmem_limit_bytes=48 * MIB),
        cost_estimate=SHORT,
        name="attend_" + mode,
    )(*inputs)


def norm_kernel(hidden, gain, ids, gates, own, *refs):
    *others, proj, out = refs
    width = hidden.shape[1]
    total = own[...].astype(jnp.float32)
    for other in others:
        total = total + other[...].astype(jnp.float32)
    rounded = total.astype(jnp.bfloat16)
    proj[...] = rounded
    residual = (hidden[...].astype(jnp.float32) + rounded.astype(jnp.float32)).astype(jnp.bfloat16)
    wide = residual.astype(jnp.float32)
    mean = jnp.mean(wide * wide, axis=1, keepdims=True)
    out[:, :width] = (wide * lax.rsqrt(mean + EPSILON) * gain[...]).astype(jnp.bfloat16)
    gate = gates[...]
    high = gate.astype(jnp.bfloat16).astype(jnp.float32)
    middle = (gate - high).astype(jnp.bfloat16).astype(jnp.float32)
    low = gate - high - middle
    spare = jnp.zeros((hidden.shape[0], out.shape[1] - width - 4 * TOP), jnp.float32)
    info = jnp.concatenate([ids[...].astype(jnp.float32), high, middle, low, spare], axis=1)
    out[:, width:] = info.astype(jnp.bfloat16)


def norm(hidden, gain, ids, gates, own, others, padded):
    tok, width = hidden.shape
    return pl.pallas_call(
        norm_kernel,
        out_shape=(
            jax.ShapeDtypeStruct((tok, width), jnp.bfloat16),
            jax.ShapeDtypeStruct((tok, padded), jnp.bfloat16),
        ),
        name="norm",
        compiler_params=pltpu.CompilerParams(vmem_limit_bytes=16 * MIB),
    )(hidden, gain.reshape(1, -1), ids, gates, own, *others)


def small(kernel, name, inputs, shapes, after):
    given = len(inputs)

    def body(*refs):
        kernel(*refs[:given], *refs[given + len(after) : -1])
        refs[-1][...] = jnp.zeros_like(refs[-1])

    moved = sum(x.size for x in inputs) + sum(x.size for x in shapes)
    return pl.pallas_call(
        body,
        out_shape=tuple(shapes) + (TOKEN,),
        in_specs=[pl.BlockSpec(memory_space=VMEM)] * given
        + [pl.BlockSpec(memory_space=pl.ANY)] * len(after),
        out_specs=tuple([pl.BlockSpec(memory_space=VMEM)] * (len(shapes) + 1)),
        compiler_params=pltpu.CompilerParams(vmem_limit_bytes=16 * MIB),
        cost_estimate=LONG,
        name=name,
    )(*inputs, *after)


def rows_like(rows, value):
    return jax.ShapeDtypeStruct((rows, value.shape[1]), value.dtype)


def assemble_kernel(*refs, plan):
    outs = refs[len(refs) - len(plan) :]
    for out, pieces in zip(outs, plan):
        at = 0
        for length, terms in pieces:
            first, start = terms[0]
            total = refs[first][start : start + length]
            if len(terms) > 1:
                total = total.astype(jnp.float32)
                for source, start in terms[1:]:
                    total = total + refs[source][start : start + length].astype(jnp.float32)
            out[at : at + length] = total.astype(out.dtype)
            at += length


def assemble(name, arrays, results, after):
    used = []
    plan = []
    for pieces in results:
        listed = []
        for length, terms in pieces:
            for key, _ in terms:
                if key not in used:
                    used.append(key)
            listed.append((length, tuple((used.index(key), start) for key, start in terms)))
        plan.append(listed)
    inputs = [arrays[key] for key in used]
    shapes = [rows_like(sum(length for length, _ in pieces), inputs[0]) for pieces in plan]
    return small(functools.partial(assemble_kernel, plan=plan), name, inputs, shapes, after)


def experts_kernel(*refs, extra):
    expert, near, far, w_in, w_down = refs[:5]
    out_near, out_far, out_last, token, rows, chosen = refs[5 + extra :]
    half, padded = near.shape
    width = w_down.shape[1]
    count = rows.shape[0] // 2
    segment = 256
    token[...] = jnp.zeros_like(token)
    earlier = (
        lax.broadcasted_iota(jnp.int32, (segment, segment), 0)
        < lax.broadcasted_iota(jnp.int32, (segment, segment), 1)
    ).astype(jnp.float32).astype(jnp.bfloat16)
    weights = []
    for side, source in enumerate((near, far)):
        info = source[:, padded - 128 :].astype(jnp.float32).T
        info = info[128 - (padded - width) :]
        named = info[:TOP] == expert[0]
        picked = jnp.sum(named.astype(jnp.float32), axis=0, keepdims=True)
        gate = info[TOP : 2 * TOP] + info[2 * TOP : 3 * TOP] + info[3 * TOP : 4 * TOP]
        weight = jnp.sum(jnp.where(named, gate, 0.0), axis=0, keepdims=True)
        base = jnp.zeros((1, 1), jnp.float32)
        slots = []
        for at in range(0, half, segment):
            one = picked[:, at : at + segment]
            eight = jnp.broadcast_to(one, (16, segment)).astype(jnp.bfloat16)
            slot = jnp.dot(eight, earlier, preferred_element_type=jnp.float32)[:1]
            slots.append(slot + base)
            base = base + jnp.sum(one, axis=1, keepdims=True)
        slot = jnp.concatenate(slots, axis=1)
        slot = jnp.where(picked > 0.5, slot, -1.0).astype(jnp.int32)
        places = lax.broadcasted_iota(jnp.int32, (count, half), 0) == slot
        chosen[side] = places.astype(jnp.float32).astype(jnp.bfloat16)
        weights.append(jnp.sum(jnp.where(places, weight, 0.0), axis=1, keepdims=True))
        got = jnp.dot(chosen[side], source[:, :width], preferred_element_type=jnp.float32)
        rows[side * count : (side + 1) * count, :] = got.astype(jnp.bfloat16)

    contract_last = (((1,), (1,)), ((), ()))
    gate = lax.dot_general(rows[...], w_in[0], contract_last, preferred_element_type=jnp.float32)
    up = lax.dot_general(rows[...], w_in[1], contract_last, preferred_element_type=jnp.float32)
    hidden = (gate / (1.0 + jnp.exp(-gate)) * up).astype(jnp.bfloat16)
    cut = out_far.shape[0]
    for side in range(2):
        here = hidden[side * count : (side + 1) * count]
        total = jnp.dot(here, w_down[...], preferred_element_type=jnp.float32)
        scaled = (total * weights[side]).astype(jnp.bfloat16)
        spread = lax.dot_general(
            chosen[side], scaled, (((0,), (0,)), ((), ())), preferred_element_type=jnp.float32
        ).astype(jnp.bfloat16)
        if side == 0:
            out_near[:, :width] = spread
        else:
            out_far[:, :width] = spread[:cut]
            out_last[:, :width] = spread[cut:]
    for target in (out_near, out_far, out_last):
        target[:, width:] = jnp.zeros((target.shape[0], padded - width), jnp.bfloat16)


def run_experts(expert, near, far, w_in, w_down, count, after=()):
    half, padded = near.shape
    width = w_down.shape[1]
    vmem = pl.BlockSpec(memory_space=VMEM)
    part = half // 4
    return pl.pallas_call(
        functools.partial(experts_kernel, extra=len(after)),
        out_shape=(
            rows_like(half, near), rows_like(half - part, near), rows_like(part, near), TOKEN
        ),
        in_specs=[pl.BlockSpec(memory_space=SMEM)]
        + [vmem] * 4
        + [pl.BlockSpec(memory_space=pl.ANY)] * len(after),
        out_specs=(vmem, vmem, vmem, vmem),
        scratch_shapes=[
            VMEM((2 * count, width), jnp.bfloat16),
            VMEM((2, count, half), jnp.bfloat16),
        ],
        compiler_params=pltpu.CompilerParams(vmem_limit_bytes=(58 if half > 256 else 30) * MIB),
        cost_estimate=SHORT,
        name="experts",
    )(expert, near, far, w_in, w_down, *after)


def plus(left, right):
    return (left.astype(jnp.float32) + right.astype(jnp.float32)).astype(jnp.bfloat16)


def last_kernel(own, *refs, starts):
    *others, out = refs
    tok, width = out.shape
    step = tok // 4
    for at in range(0, tok, step):
        total = own[at : at + step, :width].astype(jnp.float32)
        for start, other in zip(starts, others):
            if start <= at < start + other.shape[0]:
                here = slice(at - start, at - start + step)
                total = total + other[here, :width].astype(jnp.float32)
        out[at : at + step] = total.astype(jnp.bfloat16)


def per_device(
    hidden_in, qkv_new, kv_cache, cache_len, o_weight, norm_gain,
    expert_ids, gate_weights, w_gate_up, w_down,
):
    seqs = lax.axis_size("seq")
    heads = lax.axis_size("head")
    seq = lax.axis_index("seq")
    head = lax.axis_index("head")
    tok, width = hidden_in.shape
    kv_heads, lanes = qkv_new.shape[1:]
    kv_local = kv_heads // heads
    hd = kv_cache.shape[3] // 2
    gs = lanes // hd - 2
    experts = w_gate_up.shape[0] * seqs
    capacity = max(2, tok * TOP * 5 // (4 * experts))
    padded = -(-(width + 4 * TOP) // 128) * 128

    def along_head(value, mask):
        pairs = [(s * heads + h, s * heads + (h ^ mask)) for s in range(seqs) for h in range(heads)]
        return lax.ppermute(value, AXES, pairs)

    def along_seq(value, mask):
        pairs = [(s * heads + h, (s ^ mask) * heads + h) for s in range(seqs) for h in range(heads)]
        return lax.ppermute(value, AXES, pairs)

    by_group = qkv_new.reshape(tok, heads, kv_local, lanes).transpose(1, 2, 0, 3)
    parts = {
        k: lax.dynamic_index_in_dim(by_group, head ^ k, 0, keepdims=False) for k in range(heads)
    }
    order = list(range(heads - 1, 0, -1))
    for k in order:
        parts[k] = along_head(parts[k], k)
    given = [parts[k] for k in range(heads)]
    cache = jnp.swapaxes(kv_cache[0], 0, 1)
    o_rows = o_weight.T

    def info(k):
        return jnp.stack([cache_len[0], head, head ^ k]).astype(jnp.int32)

    *state, token = attend(
        "start", None, info(0), parts[0], cache, None, o_rows, None, tok, hd, gs
    )
    arrived = []
    for k in order:
        partial, _ = attend(
            "whole", token, info(k), parts[k], cache, given, o_rows, None, tok, hd, gs
        )
        arrived.append(along_head(partial, k))
    own, _ = attend(
        "end", token, info(0), parts[0], cache, given, o_rows, state, tok, hd, gs
    )
    attn_proj, rows = norm(
        hidden_in, norm_gain, expert_ids, gate_weights, own, arrived, padded
    )

    w_in = jnp.transpose(w_gate_up[0], (1, 2, 0))
    expert = seq.astype(jnp.float32).reshape(1)
    plane = {0: rows, 1: along_head(rows, 1), 2: along_head(rows, 2)}
    plane[3] = along_head(plane[2], 1)

    if seqs == 8:
        count = -(-capacity * (seqs // 2) // 16) * 16
        half = tok // 2
        x_at, y_at, low_at, high_at = tok, 2 * tok, 3 * tok, 3 * tok + half
        sequence = [0, 2, 3, 1]
        got = {f"p{i}": plane[k] for i, k in enumerate(sequence)}
        far = {}
        w_local = w_down[0]
        latest = [jnp.zeros(TOKEN.shape, TOKEN.dtype)]

        def exchange(stage, to_x, to_y):
            got[f"x{stage}"] = along_seq(to_x, 2)
            got[f"y{stage}"] = along_seq(to_y, 4)

        def run(name, results):
            *made, latest[0] = assemble(name, got, results, latest)
            del latest[1:]
            return made

        def send(name, stage, to_x, to_y, *results):
            made = run(name, [to_x, to_y, *results])
            exchange(stage, made[0], made[1])
            return made[2:]

        def experts_of(k):
            got[f"b{k}"], rest, corner, latest[0] = run_experts(
                expert, got[f"n{k}"], far[k], w_in, w_local, count, latest
            )
            got[f"r{k}"] = along_seq(rest, 1)
            got[f"c{k}"] = along_seq(corner, 1)

        def summed(k, start, length, *more):
            other = (f"r{k}", start) if start < low_at else (f"c{k}", start - low_at)
            return (length, [(f"b{k}", start), other, *more])

        def corner_of(stage, at):
            return [(half, [(f"y{stage}", at)]), (half, [(f"x{stage}", at)])]

        def pack(k, corner):
            pieces = [(tok, [(f"{name}{k}", 0)]) for name in "pxy"] + corner
            (got[f"n{k}"],) = run("pack", [pieces])
            far[k] = along_seq(got[f"n{k}"], 1)

        def returned(k, stage, at):
            return (
                [summed(k, x_at, half, (f"y{stage}", at)), summed(k, x_at + half, half)],
                [summed(k, y_at, half), summed(k, y_at + half, half, (f"x{stage}", at))],
            )

        def finished(k, stage, at=0, length=tok):
            return [summed(k, at, length, (f"x{stage}", at), (f"y{stage}", at))]

        exchange(0, rows, rows)
        latest.append(got["p3"])
        send(
            "gather", 1,
            [(tok, [("p1", 0)]), (half, [("y0", half)])],
            [(tok, [("p1", 0)]), (half, [("x0", 0)])],
        )
        neighbour_x = along_head(got["x0"], 1)
        (corner,) = send(
            "gather", 2,
            [(tok, [("p2", 0)]), (half, [("y1", half)])],
            [(tok, [("p2", 0)]), (half, [("x1", 0)])],
            corner_of(1, tok),
        )
        neighbour_y = along_head(got["y0"], 1)
        pack(0, corner_of(1, tok))
        experts_of(0)
        latest += [neighbour_x, neighbour_y]
        send(
            "turn", 3,
            [(half, [("y2", half)]), summed(0, high_at, half)],
            [(half, [("x2", 0)]), summed(0, low_at, half)],
        )
        neighbour_corner = along_head(corner, 1)
        pack(1, corner_of(2, tok))
        experts_of(1)
        latest.append(neighbour_corner)
        to_x, to_y = returned(0, 3, half)
        send(
            "turn", 4, to_x + [summed(1, high_at, half)], to_y + [summed(1, low_at, half)]
        )
        pack(2, corner_of(3, 0))
        got["nx"], got["ny"], got["nc"] = neighbour_x, neighbour_y, neighbour_corner
        (got["n3"],) = run("pack", [[(tok, [(key, 0)]) for key in ("p3", "nx", "ny", "nc")]])
        far[3] = along_seq(got["n3"], 1)
        experts_of(2)
        to_x, to_y = returned(1, 4, tok)
        (own_rows,) = send(
            "reduce", 5,
            to_x + [summed(2, high_at, half)],
            to_y + [summed(2, low_at, half)],
            finished(0, 4),
        )
        experts_of(3)
        to_x, to_y = returned(2, 5, tok)
        cut = 3 * tok // 4
        made = send(
            "reduce", 6,
            to_x + [summed(3, high_at, half)],
            to_y + [summed(3, low_at, half)],
            finished(1, 5, 0, cut),
            finished(1, 5, cut, tok - cut),
        )
        others = [(0, along_head(made[0], sequence[1])), (cut, along_head(made[1], sequence[1]))]
        latest.append(others[0][1])
        to_x, to_y = returned(3, 6, tok)
        (made,) = send("reduce", 7, to_x, to_y, finished(2, 6))
        others.append((0, along_head(made, sequence[2])))
        (made,) = run("reduce", [finished(3, 7)])
        others.append((0, along_head(made, sequence[3])))
    else:
        masks = [1 << b for b in range(1, seqs.bit_length() - 1)]
        count = -(-capacity * (seqs // 2) // 16) * 16
        done = []
        for k in range(4):
            near = plane[k]
            for mask in masks:
                near = jnp.concatenate([near, along_seq(near, mask)], axis=0)
            far = along_seq(near, 1)
            near, far, rest, _ = run_experts(expert, near, far, w_in, w_down[0], count)
            far = jnp.concatenate([far, rest], axis=0)
            near = plus(near, along_seq(far, 1))
            for mask in masks[::-1]:
                cut = near.shape[0] // 2
                near = plus(near[:cut], along_seq(near[cut:], mask))
            done.append(near)
        own_rows = done[0]
        others = [(0, along_head(done[k], k)) for k in range(1, heads)]
    moe = pl.pallas_call(
        functools.partial(last_kernel, starts=[at for at, _ in others]),
        out_shape=jax.ShapeDtypeStruct((tok, width), jnp.bfloat16),
        name="last",
    )(own_rows, *[value for _, value in others])
    return attn_proj, moe


def solution(mesh):
    return jax.shard_map(
        per_device,
        mesh=mesh,
        in_specs=(
            P(("seq", "head"), None),
            P(("seq", "head"), None, None),
            P("seq", None, "head", None),
            P("seq"),
            P("head", None),
            P(),
            P(("seq", "head"), None),
            P(("seq", "head"), None),
            P("seq", None, None, "head"),
            P("seq", "head", None),
        ),
        out_specs=(P(("seq", "head"), None), P(("seq", "head"), None)),
        check_vma=False,
    )
```

```python
import functools

import jax
import jax.numpy as jnp
from jax import lax
from jax.experimental import pallas as pl
from jax.experimental.pallas import tpu as pltpu
from jax.sharding import PartitionSpec as P

TOP = 4
EPSILON = 1e-05
LOG2E = 1.4426950408889634
FLOOR = -1e30
AXES = ("seq", "head")
MIB = 2**20
TOKEN = jax.ShapeDtypeStruct((8, 128), jnp.float32)
VMEM = pltpu.VMEM
LONG = pl.CostEstimate(flops=2 * 10**10, bytes_accessed=10**8, transcendentals=0)
SHORT = pl.CostEstimate(flops=1, bytes_accessed=1, transcendentals=0)
SMEM = pltpu.SMEM


def key_block(cached):
    return 2048 if cached % 2048 == 0 else cached


def attend_kernel(*refs, tok, hd, gs, bk, cached, mode):
    refs = list(refs)
    if mode != "start":
        refs.pop(0)
    info = refs.pop(0)
    chunk = refs.pop(0)
    cache_far = refs.pop(0)
    if mode != "start":
        parts = [refs.pop(0) for _ in range(4)]
        o_weight = refs.pop(0)
    if mode == "end":
        acc_in, top_in = refs.pop(0), refs.pop(0)
    if mode == "start":
        acc, top, token = refs.pop(0), refs.pop(0), refs.pop(0)
        queries, cache, sems = refs
    else:
        out, token = refs.pop(0), refs.pop(0)
        acc, top, queries, cache, o_local, sems = refs
    token[...] = jnp.zeros_like(token)
    heads = cache.shape[0]
    blocks = cached // bk
    live, mine, asked = info[0], info[1], info[2]
    last = (live - 1) // bk

    def cache_copy(index):
        here = pl.ds(pl.multiple_of(index * bk, bk), bk)
        return pltpu.make_async_copy(cache_far.at[:, here], cache.at[:, here], sems.at[index])

    def begin(index, carry):
        cache_copy(index).start()
        return carry

    first_block = last if mode == "end" else 0
    lax.fori_loop(first_block, last if mode == "start" else last + 1, begin, 0)
    if mode != "start":
        o_copy = pltpu.make_async_copy(o_weight, o_local, sems.at[blocks])
    for h in range(heads):
        for r in range(gs):
            one = chunk[h, :, r * hd : (r + 1) * hd] * jnp.bfloat16(hd**-0.5)
            queries[h, r * tok : (r + 1) * tok, :] = jnp.concatenate(
                [one, jnp.zeros_like(one)], axis=1
            )
    lane = lax.broadcasted_iota(jnp.int32, (1, 2 * hd), 1)
    is_value = (lane >= hd).astype(jnp.float32).astype(jnp.bfloat16)
    is_key = (lane < hd).astype(jnp.float32).astype(jnp.bfloat16)
    if mode == "end":
        acc[...] = acc_in[...]
        top[...] = top_in[...]
    elif mode == "start":
        acc[...] = jnp.zeros_like(acc)
        top[...] = jnp.full_like(top, FLOOR)

    def block(h, keys, mask):
        scores = lax.dot_general(
            queries[h], keys, (((1,), (1,)), ((), ())), preferred_element_type=jnp.float32
        )
        if mask is not None:
            scores = jnp.where(mask(scores.shape), scores, FLOOR)
        return scores

    def absorb(h, keys, scores, empty=False):
        values = keys * is_value + is_key
        largest = jnp.max(scores, axis=1, keepdims=True)
        if empty:
            now = jnp.broadcast_to(largest, top.shape[1:])
        else:
            before = top[h]
            now = jnp.maximum(before, largest)
        weights = jnp.exp2((scores - now[:, :1]) * LOG2E).astype(jnp.bfloat16)
        part = jnp.dot(weights, values, preferred_element_type=jnp.float32)
        acc[h] = part if empty else acc[h] * jnp.exp2((before - now) * LOG2E) + part
        top[h] = now

    def causal(shape):
        column = lax.broadcasted_iota(jnp.int32, shape, 1)
        row = lax.broadcasted_iota(jnp.int32, shape, 0)
        where = (mine ^ (column // tok)) * tok + column % tok
        return where <= asked * tok + row % tok

    def new_keys():
        fresh = [
            jnp.concatenate([part[h, :, gs * hd :] for part in parts], axis=0)
            for h in range(heads)
        ]
        scores = [block(h, fresh[h], causal) for h in range(heads)]
        for h in range(heads):
            absorb(h, fresh[h], scores[h], mode == "whole")

    def cached_step(index, masked):
        start = pl.multiple_of(index * bk, bk)
        cache_copy(index).wait()
        keys = [cache[h, pl.ds(start, bk), :] for h in range(heads)]

        def alive(shape):
            return lax.broadcasted_iota(jnp.int32, shape, 1) + start < live

        scores = [block(h, keys[h], alive if masked else None) for h in range(heads)]
        for h in range(heads):
            absorb(h, keys[h], scores[h])

    def body(index, carry):
        cached_step(index, False)
        return carry

    if mode != "start":
        new_keys()
        o_copy.start()
    full = last if mode == "start" else live // bk
    lax.fori_loop(first_block, full, body, 0)
    if mode == "start":
        return

    @pl.when(full * bk < live)
    def _():
        cached_step(full, True)

    pieces = []
    for h in range(heads):
        total = acc[h]
        done = (total[:, hd:] / total[:, :hd]).astype(jnp.bfloat16)
        pieces += [done[r * tok : (r + 1) * tok] for r in range(gs)]
    attention = jnp.concatenate(pieces, axis=1)
    o_copy.wait()
    turned = lax.dot_general(
        o_local[...], attention, (((1,), (1,)), ((), ())), preferred_element_type=jnp.float32
    )
    out[...] = turned.T.astype(out.dtype)


def attend(mode, after, info, chunk, cache, parts, o_rows, state, tok, hd, gs):
    heads, cached, lanes = cache.shape
    width, depth = o_rows.shape
    bk = key_block(cached)
    vmem = pl.BlockSpec(memory_space=VMEM)
    anywhere = pl.BlockSpec(memory_space=pl.ANY)
    inputs, specs = [info, chunk, cache], [pl.BlockSpec(memory_space=SMEM), vmem, anywhere]
    if mode != "start":
        inputs += [*parts, o_rows]
        specs += [vmem] * 4 + [anywhere]
    if mode == "end":
        inputs += list(state)
        specs += [vmem] * 2
    if mode != "start":
        inputs, specs = [after] + inputs, [anywhere] + specs
    held = (heads, tok * gs, lanes)
    state_shape = jax.ShapeDtypeStruct(held, jnp.float32)
    scratch = [
        VMEM(held, jnp.bfloat16),
        VMEM(cache.shape, jnp.bfloat16),
        pltpu.SemaphoreType.DMA((cached // bk + 1,)),
    ]
    if mode != "start":
        scratch = [VMEM(held, jnp.float32)] * 2 + scratch
        scratch.insert(4, VMEM((width, depth), jnp.bfloat16))
    return pl.pallas_call(
        functools.partial(
            attend_kernel, tok=tok, hd=hd, gs=gs, bk=bk, cached=cached, mode=mode
        ),
        out_shape=(state_shape, state_shape, TOKEN)
        if mode == "start"
        else (jax.ShapeDtypeStruct((tok, width), jnp.bfloat16), TOKEN),
        in_specs=specs,
        out_specs=(vmem,) * (3 if mode == "start" else 2),
        scratch_shapes=scratch,
        compiler_params=pltpu.CompilerParams(vmem_limit_bytes=48 * MIB),
        cost_estimate=SHORT,
        name="attend_" + mode,
    )(*inputs)


def norm_kernel(hidden, gain, ids, gates, own, *refs):
    *others, proj, out = refs
    width = hidden.shape[1]
    total = own[...].astype(jnp.float32)
    for other in others:
        total = total + other[...].astype(jnp.float32)
    rounded = total.astype(jnp.bfloat16)
    proj[...] = rounded
    residual = (hidden[...].astype(jnp.float32) + rounded.astype(jnp.float32)).astype(jnp.bfloat16)
    wide = residual.astype(jnp.float32)
    mean = jnp.mean(wide * wide, axis=1, keepdims=True)
    out[:, :width] = (wide * lax.rsqrt(mean + EPSILON) * gain[...]).astype(jnp.bfloat16)
    gate = gates[...]
    high = gate.astype(jnp.bfloat16).astype(jnp.float32)
    middle = (gate - high).astype(jnp.bfloat16).astype(jnp.float32)
    low = gate - high - middle
    spare = jnp.zeros((hidden.shape[0], out.shape[1] - width - 4 * TOP), jnp.float32)
    info = jnp.concatenate([ids[...].astype(jnp.float32), high, middle, low, spare], axis=1)
    out[:, width:] = info.astype(jnp.bfloat16)


def norm(hidden, gain, ids, gates, own, others, padded):
    tok, width = hidden.shape
    return pl.pallas_call(
        norm_kernel,
        out_shape=(
            jax.ShapeDtypeStruct((tok, width), jnp.bfloat16),
            jax.ShapeDtypeStruct((tok, padded), jnp.bfloat16),
        ),
        name="norm",
        compiler_params=pltpu.CompilerParams(vmem_limit_bytes=16 * MIB),
    )(hidden, gain.reshape(1, -1), ids, gates, own, *others)


def small(kernel, name, inputs, shapes, after):
    given = len(inputs)

    def body(*refs):
        kernel(*refs[:given], *refs[given + len(after) : -1])
        refs[-1][...] = jnp.zeros_like(refs[-1])

    moved = sum(x.size for x in inputs) + sum(x.size for x in shapes)
    return pl.pallas_call(
        body,
        out_shape=tuple(shapes) + (TOKEN,),
        in_specs=[pl.BlockSpec(memory_space=VMEM)] * given
        + [pl.BlockSpec(memory_space=pl.ANY)] * len(after),
        out_specs=tuple([pl.BlockSpec(memory_space=VMEM)] * (len(shapes) + 1)),
        compiler_params=pltpu.CompilerParams(vmem_limit_bytes=16 * MIB),
        cost_estimate=LONG,
        name=name,
    )(*inputs, *after)


def rows_like(rows, value):
    return jax.ShapeDtypeStruct((rows, value.shape[1]), value.dtype)


def assemble_kernel(*refs, plan):
    outs = refs[len(refs) - len(plan) :]
    for out, pieces in zip(outs, plan):
        at = 0
        for length, terms in pieces:
            first, start = terms[0]
            total = refs[first][start : start + length]
            if len(terms) > 1:
                total = total.astype(jnp.float32)
                for source, start in terms[1:]:
                    total = total + refs[source][start : start + length].astype(jnp.float32)
            out[at : at + length] = total.astype(out.dtype)
            at += length


def assemble(name, arrays, results, after):
    used = []
    plan = []
    for pieces in results:
        listed = []
        for length, terms in pieces:
            for key, _ in terms:
                if key not in used:
                    used.append(key)
            listed.append((length, tuple((used.index(key), start) for key, start in terms)))
        plan.append(listed)
    inputs = [arrays[key] for key in used]
    shapes = [rows_like(sum(length for length, _ in pieces), inputs[0]) for pieces in plan]
    return small(functools.partial(assemble_kernel, plan=plan), name, inputs, shapes, after)


def experts_kernel(*refs, extra):
    expert, near, far, w_in, w_down = refs[:5]
    out_near, out_far, out_last, token, rows, chosen = refs[5 + extra :]
    half, padded = near.shape
    width = w_down.shape[1]
    count = rows.shape[0] // 2
    segment = 256
    token[...] = jnp.zeros_like(token)
    earlier = (
        lax.broadcasted_iota(jnp.int32, (segment, segment), 0)
        < lax.broadcasted_iota(jnp.int32, (segment, segment), 1)
    ).astype(jnp.float32).astype(jnp.bfloat16)
    weights = []
    for side, source in enumerate((near, far)):
        info = source[:, padded - 128 :].astype(jnp.float32).T
        info = info[128 - (padded - width) :]
        named = info[:TOP] == expert[0]
        picked = jnp.sum(named.astype(jnp.float32), axis=0, keepdims=True)
        gate = info[TOP : 2 * TOP] + info[2 * TOP : 3 * TOP] + info[3 * TOP : 4 * TOP]
        weight = jnp.sum(jnp.where(named, gate, 0.0), axis=0, keepdims=True)
        base = jnp.zeros((1, 1), jnp.float32)
        slots = []
        for at in range(0, half, segment):
            one = picked[:, at : at + segment]
            eight = jnp.broadcast_to(one, (16, segment)).astype(jnp.bfloat16)
            slot = jnp.dot(eight, earlier, preferred_element_type=jnp.float32)[:1]
            slots.append(slot + base)
            base = base + jnp.sum(one, axis=1, keepdims=True)
        slot = jnp.concatenate(slots, axis=1)
        slot = jnp.where(picked > 0.5, slot, -1.0).astype(jnp.int32)
        places = lax.broadcasted_iota(jnp.int32, (count, half), 0) == slot
        chosen[side] = places.astype(jnp.float32).astype(jnp.bfloat16)
        weights.append(jnp.sum(jnp.where(places, weight, 0.0), axis=1, keepdims=True))
        got = jnp.dot(chosen[side], source[:, :width], preferred_element_type=jnp.float32)
        rows[side * count : (side + 1) * count, :] = got.astype(jnp.bfloat16)

    contract_last = (((1,), (1,)), ((), ()))
    gate = lax.dot_general(rows[...], w_in[0], contract_last, preferred_element_type=jnp.float32)
    up = lax.dot_general(rows[...], w_in[1], contract_last, preferred_element_type=jnp.float32)
    hidden = (gate / (1.0 + jnp.exp(-gate)) * up).astype(jnp.bfloat16)
    cut = out_far.shape[0]
    for side in range(2):
        here = hidden[side * count : (side + 1) * count]
        total = jnp.dot(here, w_down[...], preferred_element_type=jnp.float32)
        scaled = (total * weights[side]).astype(jnp.bfloat16)
        spread = lax.dot_general(
            chosen[side], scaled, (((0,), (0,)), ((), ())), preferred_element_type=jnp.float32
        ).astype(jnp.bfloat16)
        if side == 0:
            out_near[:, :width] = spread
        else:
            out_far[:, :width] = spread[:cut]
            out_last[:, :width] = spread[cut:]
    for target in (out_near, out_far, out_last):
        target[:, width:] = jnp.zeros((target.shape[0], padded - width), jnp.bfloat16)


def run_experts(expert, near, far, w_in, w_down, count, after=()):
    half, padded = near.shape
    width = w_down.shape[1]
    vmem = pl.BlockSpec(memory_space=VMEM)
    part = half // 4
    return pl.pallas_call(
        functools.partial(experts_kernel, extra=len(after)),
        out_shape=(
            rows_like(half, near), rows_like(half - part, near), rows_like(part, near), TOKEN
        ),
        in_specs=[pl.BlockSpec(memory_space=SMEM)]
        + [vmem] * 4
        + [pl.BlockSpec(memory_space=pl.ANY)] * len(after),
        out_specs=(vmem, vmem, vmem, vmem),
        scratch_shapes=[
            VMEM((2 * count, width), jnp.bfloat16),
            VMEM((2, count, half), jnp.bfloat16),
        ],
        compiler_params=pltpu.CompilerParams(vmem_limit_bytes=(58 if half > 256 else 30) * MIB),
        cost_estimate=SHORT,
        name="experts",
    )(expert, near, far, w_in, w_down, *after)


def plus(left, right):
    return (left.astype(jnp.float32) + right.astype(jnp.float32)).astype(jnp.bfloat16)


def last_kernel(own, *refs, starts):
    *others, out = refs
    tok, width = out.shape
    step = tok // 4
    for at in range(0, tok, step):
        total = own[at : at + step, :width].astype(jnp.float32)
        for start, other in zip(starts, others):
            if start <= at < start + other.shape[0]:
                here = slice(at - start, at - start + step)
                total = total + other[here, :width].astype(jnp.float32)
        out[at : at + step] = total.astype(jnp.bfloat16)


def per_device(
    hidden_in, qkv_new, kv_cache, cache_len, o_weight, norm_gain,
    expert_ids, gate_weights, w_gate_up, w_down,
):
    seqs = lax.axis_size("seq")
    heads = lax.axis_size("head")
    seq = lax.axis_index("seq")
    head = lax.axis_index("head")
    tok, width = hidden_in.shape
    kv_heads, lanes = qkv_new.shape[1:]
    kv_local = kv_heads // heads
    hd = kv_cache.shape[3] // 2
    gs = lanes // hd - 2
    experts = w_gate_up.shape[0] * seqs
    capacity = max(2, tok * TOP * 5 // (4 * experts))
    padded = -(-(width + 4 * TOP) // 128) * 128

    def along_head(value, mask):
        pairs = [(s * heads + h, s * heads + (h ^ mask)) for s in range(seqs) for h in range(heads)]
        return lax.ppermute(value, AXES, pairs)

    def along_seq(value, mask):
        pairs = [(s * heads + h, (s ^ mask) * heads + h) for s in range(seqs) for h in range(heads)]
        return lax.ppermute(value, AXES, pairs)

    by_group = qkv_new.reshape(tok, heads, kv_local, lanes).transpose(1, 2, 0, 3)
    parts = {
        k: lax.dynamic_index_in_dim(by_group, head ^ k, 0, keepdims=False) for k in range(heads)
    }
    order = list(range(heads - 1, 0, -1))
    for k in order:
        parts[k] = along_head(parts[k], k)
    given = [parts[k] for k in range(heads)]
    cache = jnp.swapaxes(kv_cache[0], 0, 1)
    o_rows = o_weight.T

    def info(k):
        return jnp.stack([cache_len[0], head, head ^ k]).astype(jnp.int32)

    *state, token = attend(
        "start", None, info(0), parts[0], cache, None, o_rows, None, tok, hd, gs
    )
    arrived = []
    for k in order:
        partial, _ = attend(
            "whole", token, info(k), parts[k], cache, given, o_rows, None, tok, hd, gs
        )
        arrived.append(along_head(partial, k))
    own, _ = attend(
        "end", token, info(0), parts[0], cache, given, o_rows, state, tok, hd, gs
    )
    attn_proj, rows = norm(
        hidden_in, norm_gain, expert_ids, gate_weights, own, arrived, padded
    )

    w_in = jnp.transpose(w_gate_up[0], (1, 2, 0))
    expert = seq.astype(jnp.float32).reshape(1)
    plane = {0: rows, 1: along_head(rows, 1), 2: along_head(rows, 2)}
    plane[3] = along_head(plane[2], 1)

    if seqs == 8:
        count = -(-capacity * (seqs // 2) // 16) * 16
        half = tok // 2
        x_at, y_at, low_at, high_at = tok, 2 * tok, 3 * tok, 3 * tok + half
        sequence = [0, 2, 3, 1]
        got = {f"p{i}": plane[k] for i, k in enumerate(sequence)}
        far = {}
        w_local = w_down[0]
        latest = [jnp.zeros(TOKEN.shape, TOKEN.dtype)]

        def exchange(stage, to_x, to_y):
            got[f"x{stage}"] = along_seq(to_x, 2)
            got[f"y{stage}"] = along_seq(to_y, 4)

        def run(name, results):
            *made, latest[0] = assemble(name, got, results, latest)
            del latest[1:]
            return made

        def send(name, stage, to_x, to_y, *results):
            made = run(name, [to_x, to_y, *results])
            exchange(stage, made[0], made[1])
            return made[2:]

        def experts_of(k):
            got[f"b{k}"], rest, corner, latest[0] = run_experts(
                expert, got[f"n{k}"], far[k], w_in, w_local, count, latest
            )
            got[f"r{k}"] = along_seq(rest, 1)
            got[f"c{k}"] = along_seq(corner, 1)

        def summed(k, start, length, *more):
            other = (f"r{k}", start) if start < low_at else (f"c{k}", start - low_at)
            return (length, [(f"b{k}", start), other, *more])

        def corner_of(stage, at):
            return [(half, [(f"y{stage}", at)]), (half, [(f"x{stage}", at)])]

        def pack(k, corner):
            pieces = [(tok, [(f"{name}{k}", 0)]) for name in "pxy"] + corner
            (got[f"n{k}"],) = run("pack", [pieces])
            far[k] = along_seq(got[f"n{k}"], 1)

        def returned(k, stage, at):
            return (
                [summed(k, x_at, half, (f"y{stage}", at)), summed(k, x_at + half, half)],
                [summed(k, y_at, half), summed(k, y_at + half, half, (f"x{stage}", at))],
            )

        def finished(k, stage, at=0, length=tok):
            return [summed(k, at, length, (f"x{stage}", at), (f"y{stage}", at))]

        exchange(0, rows, rows)
        latest.append(got["p3"])
        send(
            "gather", 1,
            [(tok, [("p1", 0)]), (half, [("y0", half)])],
            [(tok, [("p1", 0)]), (half, [("x0", 0)])],
        )
        neighbour_x = along_head(got["x0"], 1)
        (corner,) = send(
            "gather", 2,
            [(tok, [("p2", 0)]), (half, [("y1", half)])],
            [(tok, [("p2", 0)]), (half, [("x1", 0)])],
            corner_of(1, tok),
        )
        neighbour_y = along_head(got["y0"], 1)
        pack(0, corner_of(1, tok))
        experts_of(0)
        latest += [neighbour_x, neighbour_y]
        send(
            "turn", 3,
            [(half, [("y2", half)]), summed(0, high_at, half)],
            [(half, [("x2", 0)]), summed(0, low_at, half)],
        )
        neighbour_corner = along_head(corner, 1)
        pack(1, corner_of(2, tok))
        experts_of(1)
        latest.append(neighbour_corner)
        to_x, to_y = returned(0, 3, half)
        send(
            "turn", 4, to_x + [summed(1, high_at, half)], to_y + [summed(1, low_at, half)]
        )
        pack(2, corner_of(3, 0))
        got["nx"], got["ny"], got["nc"] = neighbour_x, neighbour_y, neighbour_corner
        (got["n3"],) = run("pack", [[(tok, [(key, 0)]) for key in ("p3", "nx", "ny", "nc")]])
        far[3] = along_seq(got["n3"], 1)
        experts_of(2)
        to_x, to_y = returned(1, 4, tok)
        (own_rows,) = send(
            "reduce", 5,
            to_x + [summed(2, high_at, half)],
            to_y + [summed(2, low_at, half)],
            finished(0, 4),
        )
        experts_of(3)
        to_x, to_y = returned(2, 5, tok)
        cut = 3 * tok // 4
        made = send(
            "reduce", 6,
            to_x + [summed(3, high_at, half)],
            to_y + [summed(3, low_at, half)],
            finished(1, 5, 0, cut),
            finished(1, 5, cut, tok - cut),
        )
        others = [(0, along_head(made[0], sequence[1])), (cut, along_head(made[1], sequence[1]))]
        latest.append(others[0][1])
        to_x, to_y = returned(3, 6, tok)
        (made,) = send("reduce", 7, to_x, to_y, finished(2, 6))
        others.append((0, along_head(made, sequence[2])))
        (made,) = run("reduce", [finished(3, 7)])
        others.append((0, along_head(made, sequence[3])))
    else:
        masks = [1 << b for b in range(1, seqs.bit_length() - 1)]
        count = -(-capacity * (seqs // 2) // 16) * 16
        done = []
        for k in range(4):
            near = plane[k]
            for mask in masks:
                near = jnp.concatenate([near, along_seq(near, mask)], axis=0)
            far = along_seq(near, 1)
            near, far, rest, _ = run_experts(expert, near, far, w_in, w_down[0], count)
            far = jnp.concatenate([far, rest], axis=0)
            near = plus(near, along_seq(far, 1))
            for mask in masks[::-1]:
                cut = near.shape[0] // 2
                near = plus(near[:cut], along_seq(near[cut:], mask))
            done.append(near)
        own_rows = done[0]
        others = [(0, along_head(done[k], k)) for k in range(1, heads)]
    moe = pl.pallas_call(
        functools.partial(last_kernel, starts=[at for at, _ in others]),
        out_shape=jax.ShapeDtypeStruct((tok, width), jnp.bfloat16),
        name="last",
    )(own_rows, *[value for _, value in others])
    return attn_proj, moe


def solution(mesh):
    return jax.shard_map(
        per_device,
        mesh=mesh,
        in_specs=(
            P(("seq", "head"), None),
            P(("seq", "head"), None, None),
            P("seq", None, "head", None),
            P("seq"),
            P("head", None),
            P(),
            P(("seq", "head"), None),
            P(("seq", "head"), None),
            P("seq", None, None, "head"),
            P("seq", "head", None),
        ),
        out_specs=(P(("seq", "head"), None), P(("seq", "head"), None)),
        check_vma=False,
    )
```
